512 devices in a mesh: replica: 64 (over x, z_hi, y), tensor: 8 (over z_lo, core).
Axes of the slice: x: 4, y: 4, z: 16 (z_hi: 4, z_lo: 4; z = z_hi * 4 + z_lo), core: 2. Of those that a mesh axis runs over, the one named last changes fastest.
Arguments:
- w_gate: bfloat16 [64, 1024, 3072], P('replica', None, 'tensor'), may hold values from -6 to 6
- w_up: bfloat16 [64, 1024, 3072], P('replica', None, 'tensor'), may hold values from -6 to 6
- w_down: bfloat16 [64, 3072, 1024], P('replica', 'tensor'), may hold values from -6 to 6
- pool: bfloat16 [64, 512, 1024], P('replica', None, 'tensor'), may hold values from -6 to 6
- rows_index: int32 [64, 2, 2, 128], P('replica'), may hold values from 0 to 511
- partners: int32 [2, 64], replicated, may hold values from 0 to 63, as said below
Outputs:
- new_gate: bfloat16 [64, 1024, 3072], P('replica', None, 'tensor')
- new_up: bfloat16 [64, 1024, 3072], P('replica', None, 'tensor')
- new_down: bfloat16 [64, 3072, 1024], P('replica', 'tensor')
The draws below stay inside these ranges and needn't reach their ends.
Inputs may be any that keep to these rules, and one draw needn't show every extreme that they name: Each row pairs the 64 replicas: partners[r, partners[r, i]] equals i and partners[r, i] differs from i.
All inputs are finite; a program needn't handle non-finite values.
Results may differ from the reference program's by a relative error of at most 0.029.
Values may be sent and summed in bfloat16 or wider, within the bound.
No kernel may reach another device: no remote copies, remote signals or barrier semaphores. Data moves between devices by JAX's collectives and lax.ppermute only.
A program may use at most 128 MiB of HBM per device.

```python
import jax
import jax.numpy as jnp
from jax import lax

D = 1024
FF = 3072
ROWS = 128
ROUNDS = 2
POOL = 512
REPLICAS = 64
N_TENSOR = 8


def draw_partners(key, part):
    matchings = []
    for outer_step in range(ROUNDS):
        shuffled = jax.random.permutation(jax.random.fold_in(key, 17 + outer_step), REPLICAS).astype(jnp.int32)
        first_half = shuffled[0::2]
        second_half = shuffled[1::2]
        paired = jnp.zeros((REPLICAS,), jnp.int32).at[first_half].set(second_half).at[second_half].set(first_half)
        matchings.append(paired)
    return jnp.stack(matchings)


def with_ends(entries, key, smallest, top_value):
    longest = entries.shape.index(max(entries.shape))
    spots = []
    for shift in (0, 1):
        where = [jax.random.randint(jax.random.fold_in(key, axis), (), 0, length) for axis, length in enumerate(entries.shape)]
        where[longest] = (where[longest] + shift) % entries.shape[longest]
        spots.append(tuple(where))
    return entries.at[spots[0]].set(smallest).at[spots[1]].set(top_value)


def shard_levels(own_key, dims, cuts, smallest, largest):
    loudness = 1.0
    for dim, blocks in cuts:
        heights = jax.random.uniform(jax.random.fold_in(jax.random.fold_in(own_key, 6), dim), (blocks,), jnp.float32, smallest / len(cuts), largest / len(cuts))
        loudness = loudness * jnp.repeat(jnp.exp(heights), dims[dim] // blocks).reshape((-1,) + (1,) * (len(dims) - 1 - dim))
    return loudness


def noise(stream_key, dims, width, reach, cuts=(), kind=jnp.bfloat16):
    loudness = shard_levels(stream_key, dims, cuts, -0.22, 0.18) if cuts else 1.0
    result = jax.random.normal(stream_key, dims, jnp.float32) * width * loudness
    return jnp.minimum(jnp.maximum(result, -reach), reach).astype(kind)


def setup_inputs(seed: int = 0) -> dict:
    key_list = jax.random.split(jax.random.key(seed), 7)
    return {
        "w_gate": noise(key_list[0], (REPLICAS, D, FF), 1.0, 6.0, ((0, 64), (2, 8))),
        "w_up": noise(key_list[1], (REPLICAS, D, FF), 1.0, 6.0, ((0, 64), (2, 8))),
        "w_down": noise(key_list[2], (REPLICAS, FF, D), 1.0, 6.0, ((0, 64), (1, 8))),
        "pool": noise(key_list[3], (REPLICAS, POOL, D), 1.0, 6.0, ((0, 64), (2, 8))),
        "rows_index": with_ends(jax.random.randint(key_list[4], (REPLICAS, ROUNDS, 2, ROWS), 0, POOL), jax.random.fold_in(key_list[4], 1), 0, POOL - 1).astype(jnp.int32),
        "partners": draw_partners(jax.random.fold_in(key_list[6], 71), 0),
    }


inner_rate = 1.0
outer_rate = 0.5
momentum_rate = 0.9


def local_step(weights, pool_one, picked):
    w_gate, w_up, w_down = weights
    in_scale = D ** -0.5
    hid_scale = FF ** -0.5
    inputs = jnp.take(pool_one, picked[0].astype(jnp.int32), axis=0)
    targets = jnp.take(pool_one, picked[1].astype(jnp.int32), axis=0)
    gate_pre = jnp.dot(inputs, w_gate, preferred_element_type=jnp.float32) * in_scale
    up_value = jnp.dot(inputs, w_up, preferred_element_type=jnp.float32) * in_scale
    sigmoid_gate = jax.nn.sigmoid(gate_pre)
    active = gate_pre * sigmoid_gate
    hidden = (active * up_value).astype(jnp.bfloat16)
    grouped = hidden.reshape(ROWS, N_TENSOR, FF // N_TENSOR).astype(jnp.float32)
    down_groups = w_down.reshape(N_TENSOR, FF // N_TENSOR, D).astype(jnp.float32)
    group_terms = (jnp.einsum("rkf,kfd->krd", grouped, down_groups) * hid_scale).astype(jnp.bfloat16)
    branch = jnp.sum(group_terms.astype(jnp.float32), axis=0)
    errors = (inputs.astype(jnp.float32) + branch - targets.astype(jnp.float32)).astype(jnp.bfloat16)
    back_grad = jnp.dot(errors, w_down.T, preferred_element_type=jnp.float32) * hid_scale
    delta_gate = (back_grad * up_value * sigmoid_gate * (1.0 + gate_pre * (1.0 - sigmoid_gate))).astype(jnp.bfloat16)
    delta_up = (back_grad * active).astype(jnp.bfloat16)
    grad_gate = jnp.dot(inputs.T, delta_gate, preferred_element_type=jnp.float32) * in_scale
    grad_up = jnp.dot(inputs.T, delta_up, preferred_element_type=jnp.float32) * in_scale
    grad_down = jnp.dot(hidden.T, errors, preferred_element_type=jnp.float32) * hid_scale
    gradients = (grad_gate, grad_up, grad_down)
    return tuple((weight.astype(jnp.float32) - inner_rate * gradient).astype(jnp.bfloat16) for weight, gradient in zip(weights, gradients))


def outer_update(weight, stepped, partner_step, moment, partner_moment):
    pair_mean = 0.5 * (stepped.astype(jnp.float32) + partner_step.astype(jnp.float32))
    outer_grad = weight.astype(jnp.float32) - pair_mean
    moment_new = momentum_rate * 0.5 * (moment.astype(jnp.float32) + partner_moment.astype(jnp.float32)) + outer_grad
    updated = weight.astype(jnp.float32) - outer_rate * (momentum_rate * moment_new + outer_grad)
    return updated.astype(jnp.bfloat16), moment_new.astype(jnp.bfloat16)


def make_share(stepped, moment):
    return (0.475 * stepped.astype(jnp.float32) - 0.2025 * moment.astype(jnp.float32)).astype(jnp.bfloat16)


def final_update(weight, stepped, moment, partner_share):
    updated = 0.05 * weight.astype(jnp.float32) + 0.475 * stepped.astype(jnp.float32) - 0.2025 * moment.astype(jnp.float32) + partner_share.astype(jnp.float32)
    return updated.astype(jnp.bfloat16)


def reference(w_gate, w_up, w_down, pool, rows_index, partners):
    weights = (w_gate, w_up, w_down)
    moments = tuple(jnp.zeros_like(weight) for weight in weights)
    for outer_step in range(ROUNDS):
        def replica_step(operands):
            gate_one, up_one, down_one, pool_one, picked = operands
            return local_step((gate_one, up_one, down_one), pool_one, picked)

        stepped = lax.map(replica_step, (weights[0], weights[1], weights[2], pool, rows_index[:, outer_step]))
        partner_row = partners[outer_step]
        last_round = outer_step == ROUNDS - 1

        def replica_update(operands):
            replica_id, weight_set, moment_set, step_set = operands
            partner_id = partner_row[replica_id]
            new_weights = []
            new_moments = []
            for index_mat in range(3):
                if last_round:
                    partner_share = make_share(stepped[index_mat][partner_id], moments[index_mat][partner_id])
                    updated = final_update(weight_set[index_mat], step_set[index_mat], moment_set[index_mat], partner_share)
                    moment_new = moment_set[index_mat]
                else:
                    updated, moment_new = outer_update(weight_set[index_mat], step_set[index_mat], stepped[index_mat][partner_id], moment_set[index_mat], moments[index_mat][partner_id])
                new_weights.append(updated)
                new_moments.append(moment_new)
            return tuple(new_weights), tuple(new_moments)

        weights, moments = lax.map(replica_update, (jnp.arange(REPLICAS, dtype=jnp.int32), weights, moments, stepped))
    return weights[0], weights[1], weights[2]
```

```python
import jax
import jax.numpy as jnp
from jax import lax
from jax.experimental import pallas as pl
from jax.experimental.pallas import tpu as pltpu
from jax.sharding import Mesh, PartitionSpec as P

D = 1024
FF = 3072
REPLICAS = 64
N_TENSOR = 8
PLANE = 16
PLANES = 4
ROUNDS = 2
IN_SCALE = D**-0.5
HID_SCALE = FF**-0.5

inner_rate = 1.0
outer_rate = 0.5
momentum_rate = 0.9

REPLICA = ("x", "h", "y")
FLAT = ("x", "y")
TENSOR = ("l", "c")

NEXT_SLOTS = (5, 6, 7, 8)
FAR_SLOTS = (4, 5, 6, 8)
SLOTS = [(n, f) for n in NEXT_SLOTS for f in FAR_SLOTS] + [(PLANE, PLANE)]


def routes(partners):
    me = lax.axis_index("h")
    ids = jnp.arange(REPLICAS, dtype=jnp.int32)
    plane = (ids // 4) % PLANES
    flat = (ids // PLANE) * 4 + ids % 4
    to_plane = (partners // 4) % PLANES
    off = (to_plane - plane + PLANES) % PLANES
    same = (plane[:, None] == plane[None, :]) & (flat[None, :] < flat[:, None])
    rank = jnp.sum((same & (off[:, :, None] == off[:, None, :])).astype(jnp.int32), axis=2)
    slots = jnp.arange(PLANE, dtype=jnp.int32)
    offs = jnp.array([1, 3, 2], jnp.int32)
    here = (plane == me)[None, None, None, :]
    sends = here & (off[:, None, None, :] == offs[None, :, None, None])
    sends = sends & (rank[:, None, None, :] == slots[None, None, :, None])
    send_index = jnp.sum(jnp.where(sends, flat, 0), axis=3)
    home = (slots // 4) * PLANE + me * 4 + slots % 4
    wanted = partners[:, None, :] == home[None, :, None]
    come_from = (plane[None, :] - me + PLANES) % PLANES
    kind = jnp.sum(jnp.where(wanted, come_from[:, None, :], 0), axis=2)
    place = jnp.where(off == 0, flat[None, :], rank)
    slot = jnp.sum(jnp.where(wanted, place[:, None, :], 0), axis=2)
    most_next = jnp.max(jnp.where(off % 2 == 1, rank + 1, 0), axis=1)
    most_far = jnp.max(jnp.where(off == 2, rank + 1, 0), axis=1)
    case_next = sum((most_next > n).astype(jnp.int32) for n in NEXT_SLOTS[:-1])
    case_far = sum((most_far > n).astype(jnp.int32) for n in FAR_SLOTS[:-1])
    fits = (most_next <= NEXT_SLOTS[-1]) & (most_far <= FAR_SLOTS[-1])
    case = jnp.where(fits, case_next * len(FAR_SLOTS) + case_far, len(SLOTS) - 1)
    return case, send_index, jnp.stack([kind, slot], axis=1)


def pick_kernel(index, chunks, *rest):
    outs, sem = rest[:3], rest[3]
    copies, at = [], 0
    for o, out in enumerate(outs):
        for k in range(out.shape[0]):
            copies.append(pltpu.make_async_copy(chunks.at[index[o, k]], out.at[k], sem.at[at]))
            at += 1
    for copy in copies:
        copy.start()
    for copy in copies:
        copy.wait()


def pick(index, chunks, counts):
    anywhere = pl.BlockSpec(memory_space=pl.ANY)
    return pl.pallas_call(
        pick_kernel,
        out_shape=tuple(
            jax.ShapeDtypeStruct((n, *chunks.shape[1:]), chunks.dtype) for n in counts
        ),
        grid_spec=pltpu.PrefetchScalarGridSpec(
            num_scalar_prefetch=1,
            grid=(1,),
            in_specs=[anywhere],
            out_specs=(anywhere,) * 3,
            scratch_shapes=[pltpu.SemaphoreType.DMA((sum(counts),))],
        ),
        cost_estimate=pl.CostEstimate(
            flops=0, bytes_accessed=4 * PLANE * chunks[0].size, transcendentals=0
        ),
    )(index, chunks)


def place_kernel(where, own, ahead, behind, far, out, sem):
    sources = (own, ahead, far, behind)
    for d in range(PLANE):
        for kind, source in enumerate(sources):

            @pl.when(where[0, d] == kind)
            def _(d=d, source=source):
                pltpu.make_async_copy(source.at[where[1, d]], out.at[d], sem.at[d]).start()

    for d in range(PLANE):
        pltpu.make_async_copy(own.at[0], out.at[d], sem.at[d]).wait()


def place(where, own, ahead, behind, far):
    anywhere = pl.BlockSpec(memory_space=pl.ANY)
    return pl.pallas_call(
        place_kernel,
        out_shape=jax.ShapeDtypeStruct(own.shape, own.dtype),
        grid_spec=pltpu.PrefetchScalarGridSpec(
            num_scalar_prefetch=1,
            grid=(1,),
            in_specs=[anywhere] * 4,
            out_specs=anywhere,
            scratch_shapes=[pltpu.SemaphoreType.DMA((PLANE,))],
        ),
        cost_estimate=pl.CostEstimate(
            flops=0, bytes_accessed=4 * own.size, transcendentals=0
        ),
    )(where, own, ahead, behind, far)


def step_by(n):
    return [(i, (i + n) % PLANES) for i in range(PLANES)]


def swap(arrays, send_index, where, n_next, n_far):
    shares = [
        lax.all_to_all(a.reshape(PLANE, a.shape[0] // PLANE, a.shape[1]), FLAT, 0, 0, tiled=True)
        for a in arrays
    ]
    moved = []
    for share in shares:
        up, down, across = pick(send_index, share, (n_next, n_next, n_far))
        from_behind = lax.ppermute(up, "h", step_by(1))
        from_ahead = lax.ppermute(down, "h", step_by(-1))
        from_far = lax.ppermute(across, "h", step_by(2))
        moved.append((from_ahead, from_behind, from_far))
    got = []
    for a, share, parts in zip(arrays, shares, moved):
        placed = place(where, share, *parts)
        got.append(lax.all_to_all(placed, FLAT, 0, 0, tiled=True).reshape(a.shape))
    return tuple(got)


def partner_copy(arrays, route):
    case, send_index, where = route
    branches = [
        lambda arrays, s, w, n=n, f=f: swap(arrays, s, w, n, f) for n, f in SLOTS
    ]
    return lax.switch(case, branches, arrays, send_index, where)


def local_step(weights, inputs, in_cols, out_cols):
    w_gate, w_up, w_down = weights
    gate_pre = jnp.dot(inputs, w_gate, preferred_element_type=jnp.float32) * IN_SCALE
    up_value = jnp.dot(inputs, w_up, preferred_element_type=jnp.float32) * IN_SCALE
    sigmoid_gate = jax.nn.sigmoid(gate_pre)
    active = gate_pre * sigmoid_gate
    hidden = (active * up_value).astype(jnp.bfloat16)
    term = jnp.dot(hidden, w_down, preferred_element_type=jnp.float32) * HID_SCALE
    cols = D // N_TENSOR
    term = term.astype(jnp.bfloat16)
    blocks = jnp.stack([term[:, k * cols : (k + 1) * cols] for k in range(N_TENSOR)])
    terms = lax.all_to_all(blocks, TENSOR, 0, 0, tiled=True)
    branch = jnp.sum(terms.astype(jnp.float32), axis=0)
    error_cols = (in_cols.astype(jnp.float32) + branch - out_cols.astype(jnp.float32)).astype(
        jnp.bfloat16
    )
    errors = lax.all_gather(error_cols, TENSOR, axis=1, tiled=True)
    back = (
        lax.dot_general(
            errors, w_down, (((1,), (1,)), ((), ())), preferred_element_type=jnp.float32
        )
        * HID_SCALE
    )
    delta_gate = (back * up_value * sigmoid_gate * (1.0 + gate_pre * (1.0 - sigmoid_gate))).astype(
        jnp.bfloat16
    )
    delta_up = (back * active).astype(jnp.bfloat16)
    rows = (((0,), (0,)), ((), ()))

    def grad(a, b, scale):
        return lax.dot_general(a, b, rows, preferred_element_type=jnp.float32) * scale

    gradients = (
        grad(inputs, delta_gate, IN_SCALE),
        grad(inputs, delta_up, IN_SCALE),
        grad(hidden, errors, HID_SCALE),
    )
    return tuple(
        (w.astype(jnp.float32) - inner_rate * g).astype(jnp.bfloat16)
        for w, g in zip(weights, gradients)
    )


def outer_update(weight, stepped, partner_step):
    weight = weight.astype(jnp.float32)
    pair_mean = 0.5 * (stepped.astype(jnp.float32) + partner_step.astype(jnp.float32))
    outer_grad = weight - pair_mean
    moment_new = outer_grad
    updated = weight - outer_rate * (momentum_rate * moment_new + outer_grad)
    return updated.astype(jnp.bfloat16), moment_new.astype(jnp.bfloat16)


def make_share(stepped, moment):
    return (0.475 * stepped.astype(jnp.float32) - 0.2025 * moment.astype(jnp.float32)).astype(
        jnp.bfloat16
    )


def final_update(weight, stepped, moment, partner_share):
    updated = (
        0.05 * weight.astype(jnp.float32)
        + 0.475 * stepped.astype(jnp.float32)
        - 0.2025 * moment.astype(jnp.float32)
        + partner_share.astype(jnp.float32)
    )
    return updated.astype(jnp.bfloat16)


def body(w_gate, w_up, w_down, pool, rows_index, partners):
    weights = (w_gate[0], w_up[0], w_down[0])
    case, send_index, where = routes(partners)
    picked = jnp.take(pool[0], rows_index[0].reshape(-1), axis=0)
    picked = picked.reshape(ROUNDS, 2, -1, picked.shape[-1])
    in_cols, out_cols = picked[:, 0], picked[:, 1]
    inputs = lax.all_gather(in_cols, TENSOR, axis=2, tiled=True)

    stepped = local_step(weights, inputs[0], in_cols[0], out_cols[0])
    theirs = partner_copy(stepped, (case[0], send_index[0], where[0]))
    results = [outer_update(*each) for each in zip(weights, stepped, theirs)]
    weights = tuple(r[0] for r in results)
    moments = tuple(r[1] for r in results)

    stepped = local_step(weights, inputs[1], in_cols[1], out_cols[1])
    shares = tuple(make_share(s, m) for s, m in zip(stepped, moments))
    theirs = partner_copy(shares, (case[1], send_index[1], where[1]))
    new = [final_update(*each) for each in zip(weights, stepped, moments, theirs)]
    return tuple(w[None] for w in new)


def solution(mesh):
    grid = Mesh(mesh.devices.reshape(4, 4, 4, 4, 2), ("x", "h", "y", "l", "c"))
    return jax.shard_map(
        body,
        mesh=grid,
        in_specs=(
            P(REPLICA, None, TENSOR),
            P(REPLICA, None, TENSOR),
            P(REPLICA, TENSOR, None),
            P(REPLICA, None, TENSOR),
            P(REPLICA, None, None, None),
            P(),
        ),
        out_specs=(
            P(REPLICA, None, TENSOR),
            P(REPLICA, None, TENSOR),
            P(REPLICA, TENSOR, None),
        ),
        check_vma=False,
    )
```

```python
import functools

import jax
import jax.numpy as jnp
from jax import lax
from jax.experimental import pallas as pl
from jax.experimental.pallas import tpu as pltpu
from jax.sharding import Mesh, PartitionSpec as P

D = 1024
FF = 3072
HID = 384
REPLICAS = 64
N_TENSOR = 8
COLS = D // N_TENSOR
PLANE = 16
PLANES = 4
ROUNDS = 2
IN_SCALE = D**-0.5
HID_SCALE = FF**-0.5

inner_rate = 1.0
outer_rate = 0.5
momentum_rate = 0.9

REPLICA = ("x", "h", "y")
FLAT = ("x", "y")
TENSOR = ("l", "c")

NEXT = 6
FAR = 6
MORE = 2
VMEM = 48 << 20


def routes(partners):
    me = lax.axis_index("h")
    ids = jnp.arange(REPLICAS, dtype=jnp.int32)
    plane = (ids // 4) % PLANES
    flat = (ids // PLANE) * 4 + ids % 4
    to_plane = (partners // 4) % PLANES
    off = (to_plane - plane + PLANES) % PLANES
    same = (plane[:, None] == plane[None, :]) & (flat[None, :] < flat[:, None])
    rank = jnp.sum((same & (off[:, :, None] == off[:, None, :])).astype(jnp.int32), axis=2)
    places = jnp.arange(PLANE, dtype=jnp.int32)
    slots = jnp.arange(PLANE + 2 * MORE, dtype=jnp.int32)
    offs = jnp.array([1, 3, 2], jnp.int32)
    here = (plane == me)[None, None, None, :]
    sends = here & (off[:, None, None, :] == offs[None, :, None, None])
    sends = sends & (rank[:, None, None, :] == slots[None, None, :, None])
    send_index = jnp.sum(jnp.where(sends, flat, 0), axis=3)
    home = (places // 4) * PLANE + me * 4 + places % 4
    wanted = partners[:, None, :] == home[None, :, None]
    come_from = (plane[None, :] - me + PLANES) % PLANES
    kind = jnp.sum(jnp.where(wanted, come_from[:, None, :], 0), axis=2)
    place = jnp.where(off == 0, flat[None, :], rank)
    slot = jnp.sum(jnp.where(wanted, place[:, None, :], 0), axis=2)
    extra = jnp.where(off == 2, rank + 1 - FAR, jnp.where(off == 0, 0, rank + 1 - NEXT))
    trips = jnp.maximum((jnp.max(extra, axis=1) + MORE - 1) // MORE, 0)
    where = jnp.stack([kind, slot], axis=1)
    return [(send_index[r], where[r], trips[r]) for r in range(ROUNDS)]


def kernel_call(kernel, out_shape, index_args, args, name):
    scalars = [pl.BlockSpec(memory_space=pltpu.SMEM)] * len(index_args)
    whole = pl.BlockSpec(memory_space=pltpu.VMEM)
    size = sum(a.size * a.dtype.itemsize for a in (*args, *out_shape))
    return pl.pallas_call(
        kernel,
        out_shape=out_shape,
        in_specs=scalars + [whole] * len(args),
        out_specs=(whole,) * len(out_shape),
        compiler_params=pltpu.CompilerParams(vmem_limit_bytes=VMEM),
        cost_estimate=pl.CostEstimate(flops=size, bytes_accessed=size, transcendentals=0),
        name=name,
    )(*index_args, *args)


def pick_kernel(index, chunks, *outs):
    for o, out in enumerate(outs):

        @pl.loop(0, out.shape[0])
        def _(k, o=o, out=out):
            out[k] = chunks[index[o, k]]


def pick(index, chunks, counts):
    out_shape = tuple(jax.ShapeDtypeStruct((n, *chunks.shape[1:]), chunks.dtype) for n in counts)
    return kernel_call(pick_kernel, out_shape, (index,), (chunks,), "pick")


def merge_kernel(fn, first, n_own, n_out, where, low, *refs):
    ahead, behind, far, own = refs[:3] + (refs[3:],)
    own, before, outs = own[:n_own], own[n_own:-n_out], own[-n_out:]

    @pl.loop(0, PLANE)
    def _(d):
        kind, slot = where[0, d], where[1, d]

        def use(theirs):
            for out, value in zip(outs, fn(theirs, *(o[d] for o in own))):
                out[d] = value.astype(out.dtype)

        if not first:
            for out, old in zip(outs, before):
                out[d] = old[d]
        else:

            @pl.when(kind == 0)
            def _():
                use(own[0][slot])

        for number, source in ((1, ahead), (2, far), (3, behind)):
            at = slot - low[number // 2 % 2 if number < 3 else 0]

            @pl.when((kind == number) & (at >= 0) & (at < source.shape[0]))
            def _(source=source, at=at):
                use(source[at])


def merge(fn, where, low, arrived, own, outs, before=()):
    kernel = functools.partial(merge_kernel, fn, not before, len(own), outs)
    out_shape = (jax.ShapeDtypeStruct(own[0].shape, own[0].dtype),) * outs
    return kernel_call(kernel, out_shape, (where, low), (*arrived, *own, *before), "merge")


def step_by(n):
    return [(i, (i + n) % PLANES) for i in range(PLANES)]


def hop(index, chunks, n_next, n_far):
    up, down, across = pick(index, chunks, (n_next, n_next, n_far))
    from_far = lax.ppermute(across, "h", step_by(2))
    from_behind = lax.ppermute(up, "h", step_by(1))
    from_ahead = lax.ppermute(down, "h", step_by(-1))
    return from_ahead, from_behind, from_far


def depart(route, chunks):
    return hop(route[0], chunks, NEXT, FAR)


def arrive(route, fn, outs, arrived, own):
    send_index, where, trips = route
    low = jnp.array([NEXT, FAR], jnp.int32)
    done = [merge(fn, where, 0 * low, a, o, outs) for a, o in zip(arrived, own)]

    def late(state):
        i, done = state
        at = low + MORE * i
        index = jnp.stack(
            [lax.dynamic_slice(send_index[o], (at[o // 2],), (MORE,)) for o in range(3)]
        )
        done = [
            merge(fn, where, at, hop(index, o[0], MORE, MORE), o, outs, before=b)
            for o, b in zip(own, done)
        ]
        return i + 1, done

    return lax.while_loop(lambda s: s[0] < trips, late, (jnp.int32(0), done))[1]


def over_plane(chunks):
    return lax.all_to_all(chunks, FLAT, 0, 0, tiled=True)


def spread(a):
    return over_plane(a.reshape(PLANE, a.shape[0] // PLANE, a.shape[1]))


def back_home(chunks):
    return over_plane(chunks).reshape(-1, chunks.shape[-1])


rows = (((0,), (0,)), ((), ()))


def grad(a, b):
    return lax.dot_general(a, b, rows, preferred_element_type=jnp.float32)


def local_step(both, down, inputs, in_cols, out_cols):
    pre = jnp.dot(inputs, both, preferred_element_type=jnp.float32) * IN_SCALE
    gate_pre, up_value = pre[:, :HID], pre[:, HID:]
    sigmoid_gate = jax.nn.sigmoid(gate_pre)
    active = gate_pre * sigmoid_gate
    hidden = (active * up_value).astype(jnp.bfloat16)
    term = jnp.dot(hidden, down, preferred_element_type=jnp.float32) * HID_SCALE
    term = term.astype(jnp.bfloat16)
    blocks = term.reshape(-1, N_TENSOR, COLS).transpose(1, 0, 2)
    terms = lax.all_to_all(blocks, TENSOR, 0, 0, tiled=True)
    branch = jnp.sum(terms.astype(jnp.float32), axis=0)
    error_cols = (in_cols.astype(jnp.float32) + branch - out_cols.astype(jnp.float32)).astype(
        jnp.bfloat16
    )
    errors = lax.all_gather(error_cols, TENSOR, axis=1, tiled=True)
    back = (
        lax.dot_general(errors, down, (((1,), (1,)), ((), ())), preferred_element_type=jnp.float32)
        * HID_SCALE
    )
    delta_gate = back * up_value * sigmoid_gate * (1.0 + gate_pre * (1.0 - sigmoid_gate))
    delta_up = back * active
    deltas = jnp.concatenate([delta_gate, delta_up], axis=1).astype(jnp.bfloat16)
    return deltas, hidden, errors, error_cols


def outer_update(theirs, stepped, weight):
    weight = weight.astype(jnp.float32)
    pair_mean = 0.5 * (stepped.astype(jnp.float32) + theirs.astype(jnp.float32))
    outer_grad = weight - pair_mean
    moment = outer_grad.astype(jnp.bfloat16).astype(jnp.float32)
    updated = weight - outer_rate * (momentum_rate * outer_grad + outer_grad)
    updated = updated.astype(jnp.bfloat16)
    return updated, 0.475 * updated.astype(jnp.float32) - 0.2025 * moment


def pair_sum(theirs, own):
    return (theirs.astype(jnp.float32) + own.astype(jnp.float32),)


def partners_own(theirs, own):
    return (theirs,)


def body(w_gate, w_up, w_down, pool, rows_index, partners):
    both = jnp.concatenate([w_gate[0], w_up[0]], axis=1)
    down = w_down[0]
    first, last = routes(partners)
    picked = jnp.take(pool[0], rows_index[0].reshape(-1), axis=0)
    picked = picked.reshape(ROUNDS, 2, -1, COLS)
    in_cols, out_cols = picked[:, 0], picked[:, 1]
    inputs = lax.all_gather(in_cols, TENSOR, axis=2, tiled=True)
    start = [spread(both), spread(down)]

    deltas, hidden, errors, _ = local_step(both, down, inputs[0], in_cols[0], out_cols[0])
    step_down = (down.astype(jnp.float32) - HID_SCALE * grad(hidden, errors)).astype(jnp.bfloat16)
    step_both = (both.astype(jnp.float32) - IN_SCALE * grad(inputs[0], deltas)).astype(jnp.bfloat16)
    stepped = [spread(step_both), spread(step_down)]
    arrived = [depart(first, s) for s in stepped]
    done = arrive(first, outer_update, 2, arrived, list(zip(stepped, start)))

    shares = [share for _, share in done]
    arrived = [depart(last, s) for s in shares]
    both, down = (back_home(new) for new, _ in done)
    deltas, hidden, errors, error_cols = local_step(
        both, down, inputs[1], in_cols[1], out_cols[1]
    )
    factors = jnp.concatenate([deltas, hidden, error_cols, in_cols[1]], axis=1)
    arrived, factors = lax.optimization_barrier((arrived, factors))
    factors = spread(factors)
    on_way = depart(last, factors)
    sums = arrive(last, pair_sum, 1, arrived, [(s,) for s in shares])
    sum_both, sum_down = (back_home(s[0]) for s in sums)
    theirs = back_home(arrive(last, partners_own, 1, [on_way], [(factors,)])[0][0])
    cols = theirs[:, 3 * HID :].reshape(-1, 2, COLS).transpose(1, 0, 2)
    cols = lax.all_gather(cols, TENSOR, axis=2, tiled=True)

    def pair(mine, other):
        return jnp.concatenate([mine, other], axis=0)

    deltas = pair(deltas, theirs[:, : 2 * HID])
    hidden = pair(hidden, theirs[:, 2 * HID : 3 * HID])
    errors = pair(errors, cols[0])
    inputs = pair(inputs[1], cols[1])

    def final(weight, known, a, b, scale):
        new = 0.05 * weight.astype(jnp.float32) + known.astype(jnp.float32)
        return (new - (0.475 * inner_rate * scale) * grad(a, b)).astype(jnp.bfloat16)[None]

    return (
        final(both[:, :HID], sum_both[:, :HID], inputs, deltas[:, :HID], IN_SCALE),
        final(both[:, HID:], sum_both[:, HID:], inputs, deltas[:, HID:], IN_SCALE),
        final(down, sum_down, hidden, errors, HID_SCALE),
    )


def solution(mesh):
    grid = Mesh(mesh.devices.reshape(4, 4, 4, 4, 2), ("x", "h", "y", "l", "c"))
    return jax.shard_map(
        body,
        mesh=grid,
        in_specs=(
            P(REPLICA, None, TENSOR),
            P(REPLICA, None, TENSOR),
            P(REPLICA, TENSOR, None),
            P(REPLICA, None, TENSOR),
            P(REPLICA, None, None, None),
            P(),
        ),
        out_specs=(
            P(REPLICA, None, TENSOR),
            P(REPLICA, None, TENSOR),
            P(REPLICA, TENSOR, None),
        ),
        check_vma=False,
    )
```

```python
import functools

import jax
import jax.numpy as jnp
from jax import lax
from jax.experimental import pallas as pl
from jax.experimental.pallas import tpu as pltpu
from jax.sharding import Mesh, PartitionSpec as P

D = 1024
FF = 3072
HID = 384
REPLICAS = 64
N_TENSOR = 8
COLS = D // N_TENSOR
PLANE = 16
PLANES = 4
ROUNDS = 2
IN_SCALE = D**-0.5
HID_SCALE = FF**-0.5

inner_rate = 1.0
outer_rate = 0.5
momentum_rate = 0.9

REPLICA = ("x", "h", "y")
FLAT = ("x", "y")
TENSOR = ("l", "c")

NEXT = 6
FAR = 6
MORE = 2
VMEM = 48 << 20


def routes(partners):
    me = lax.axis_index("h")
    ids = jnp.arange(REPLICAS, dtype=jnp.int32)
    plane = (ids // 4) % PLANES
    flat = (ids // PLANE) * 4 + ids % 4
    to_plane = (partners // 4) % PLANES
    off = (to_plane - plane + PLANES) % PLANES
    same = (plane[:, None] == plane[None, :]) & (flat[None, :] < flat[:, None])
    rank = jnp.sum((same & (off[:, :, None] == off[:, None, :])).astype(jnp.int32), axis=2)
    places = jnp.arange(PLANE, dtype=jnp.int32)
    slots = jnp.arange(PLANE + 2 * MORE, dtype=jnp.int32)
    offs = jnp.array([1, 3, 2], jnp.int32)
    here = (plane == me)[None, None, None, :]
    sends = here & (off[:, None, None, :] == offs[None, :, None, None])
    sends = sends & (rank[:, None, None, :] == slots[None, None, :, None])
    send_index = jnp.sum(jnp.where(sends, flat, 0), axis=3)
    home = (places // 4) * PLANE + me * 4 + places % 4
    wanted = partners[:, None, :] == home[None, :, None]
    come_from = (plane[None, :] - me + PLANES) % PLANES
    kind = jnp.sum(jnp.where(wanted, come_from[:, None, :], 0), axis=2)
    place = jnp.where(off == 0, flat[None, :], rank)
    slot = jnp.sum(jnp.where(wanted, place[:, None, :], 0), axis=2)
    extra = jnp.where(off == 2, rank + 1 - FAR, jnp.where(off == 0, 0, rank + 1 - NEXT))
    trips = jnp.maximum((jnp.max(extra, axis=1) + MORE - 1) // MORE, 0)
    where = jnp.stack([kind, slot], axis=1)
    return [(send_index[r], where[r], trips[r]) for r in range(ROUNDS)]


def kernel_call(kernel, out_shape, index_args, args, name):
    scalars = [pl.BlockSpec(memory_space=pltpu.SMEM)] * len(index_args)
    whole = pl.BlockSpec(memory_space=pltpu.VMEM)
    size = sum(a.size * a.dtype.itemsize for a in (*args, *out_shape))
    return pl.pallas_call(
        kernel,
        out_shape=out_shape,
        in_specs=scalars + [whole] * len(args),
        out_specs=(whole,) * len(out_shape),
        compiler_params=pltpu.CompilerParams(vmem_limit_bytes=VMEM),
        cost_estimate=pl.CostEstimate(flops=size, bytes_accessed=size, transcendentals=0),
        name=name,
    )(*index_args, *args)


def pick_kernel(index, chunks, *outs):
    for o, out in enumerate(outs):

        @pl.loop(0, out.shape[0])
        def _(k, o=o, out=out):
            out[k] = chunks[index[o, k]]


def pick(index, chunks, counts):
    out_shape = tuple(jax.ShapeDtypeStruct((n, *chunks.shape[1:]), chunks.dtype) for n in counts)
    return kernel_call(pick_kernel, out_shape, (index,), (chunks,), "pick")


def merge_kernel(fn, first, n_own, n_out, where, low, *refs):
    ahead, behind, far, own = refs[:3] + (refs[3:],)
    own, before, outs = own[:n_own], own[n_own:-n_out], own[-n_out:]

    @pl.loop(0, PLANE)
    def _(d):
        kind, slot = where[0, d], where[1, d]

        def use(theirs):
            for out, value in zip(outs, fn(theirs, *(o[d] for o in own))):
                out[d] = value.astype(out.dtype)

        if not first:
            for out, old in zip(outs, before):
                out[d] = old[d]
        else:

            @pl.when(kind == 0)
            def _():
                use(own[0][slot])

        for number, source in ((1, ahead), (2, far), (3, behind)):
            at = slot - low[number // 2 % 2 if number < 3 else 0]

            @pl.when((kind == number) & (at >= 0) & (at < source.shape[0]))
            def _(source=source, at=at):
                use(source[at])


def merge(fn, where, low, arrived, own, outs, before=()):
    kernel = functools.partial(merge_kernel, fn, not before, len(own), outs)
    out_shape = (jax.ShapeDtypeStruct(own[0].shape, own[0].dtype),) * outs
    return kernel_call(kernel, out_shape, (where, low), (*arrived, *own, *before), "merge")


def step_by(n):
    return [(i, (i + n) % PLANES) for i in range(PLANES)]


def hop(sends):
    up, down, across = sends
    from_far = lax.ppermute(across, "h", step_by(2))
    from_behind = lax.ppermute(up, "h", step_by(1))
    from_ahead = lax.ppermute(down, "h", step_by(-1))
    return from_ahead, from_behind, from_far


def over_plane(chunks):
    return lax.all_to_all(chunks, FLAT, 0, 0, tiled=True)


def arrive(route, arrived, own):
    send_index, where, trips = route
    low = jnp.array([NEXT, FAR], jnp.int32)
    placed = merge(partners_own, where, 0 * low, arrived, (own,), 1)

    def late(state):
        i, placed = state
        at = low + MORE * i
        index = jnp.stack(
            [lax.dynamic_slice(send_index[o], (at[o // 2],), (MORE,)) for o in range(3)]
        )
        parts = hop(pick(index, own, (MORE,) * 3))
        return i + 1, merge(partners_own, where, at, parts, (own,), 1, before=placed)

    return lax.while_loop(lambda s: s[0] < trips, late, (jnp.int32(0), placed))[1]


def swap(route, arrays):
    arrays = [a.reshape(PLANE, a.shape[0] // PLANE, a.shape[1]) for a in arrays]
    shares, moved = [], []
    for i, a in enumerate(arrays):
        if i:
            a, _ = lax.optimization_barrier((a, shares[-1]))
        share = over_plane(a)
        sends = pick(route[0], share, (NEXT, NEXT, FAR))
        if i:
            moved[-1], _ = lax.optimization_barrier((moved[-1], sends))
        shares.append(share)
        moved.append(hop(sends))
    return [over_plane(arrive(route, m, s)[0]) for m, s in zip(moved, shares)]


rows = (((0,), (0,)), ((), ()))


def grad(a, b):
    return lax.dot_general(a, b, rows, preferred_element_type=jnp.float32)


def local_step(weights, inputs, in_cols, out_cols):
    w_gate, w_up, w_down = weights
    gate_pre = jnp.dot(inputs, w_gate, preferred_element_type=jnp.float32) * IN_SCALE
    up_value = jnp.dot(inputs, w_up, preferred_element_type=jnp.float32) * IN_SCALE
    sigmoid_gate = jax.nn.sigmoid(gate_pre)
    active = gate_pre * sigmoid_gate
    hidden = (active * up_value).astype(jnp.bfloat16)
    term = jnp.dot(hidden, w_down, preferred_element_type=jnp.float32) * HID_SCALE
    blocks = term.astype(jnp.bfloat16).reshape(-1, N_TENSOR, COLS).transpose(1, 0, 2)
    terms = lax.all_to_all(blocks, TENSOR, 0, 0, tiled=True)
    branch = jnp.sum(terms.astype(jnp.float32), axis=0)
    error_cols = (in_cols.astype(jnp.float32) + branch - out_cols.astype(jnp.float32)).astype(
        jnp.bfloat16
    )
    errors = lax.all_gather(error_cols, TENSOR, axis=1, tiled=True)
    back = (
        lax.dot_general(
            errors, w_down, (((1,), (1,)), ((), ())), preferred_element_type=jnp.float32
        )
        * HID_SCALE
    )
    delta_gate = (back * up_value * sigmoid_gate * (1.0 + gate_pre * (1.0 - sigmoid_gate))).astype(
        jnp.bfloat16
    )
    delta_up = (back * active).astype(jnp.bfloat16)
    gradients = (
        grad(inputs, delta_gate) * IN_SCALE,
        grad(inputs, delta_up) * IN_SCALE,
        grad(hidden, errors) * HID_SCALE,
    )
    return tuple(
        (w.astype(jnp.float32) - inner_rate * g).astype(jnp.bfloat16)
        for w, g in zip(weights, gradients)
    )


def partner_copy(route, arrays):
    gate, up, down = arrays
    down_in, gate_in, up_in = swap(route, [down, gate, up])
    return tuple(g.reshape(a.shape) for g, a in zip((gate_in, up_in, down_in), arrays))


def partners_own(theirs, own):
    return (theirs,)


def outer_update(weight, stepped, partner_step):
    weight = weight.astype(jnp.float32)
    pair_mean = 0.5 * (stepped.astype(jnp.float32) + partner_step.astype(jnp.float32))
    outer_grad = weight - pair_mean
    moment_new = outer_grad
    updated = weight - outer_rate * (momentum_rate * moment_new + outer_grad)
    return updated.astype(jnp.bfloat16), moment_new.astype(jnp.bfloat16)


def make_share(stepped, moment):
    return (0.475 * stepped.astype(jnp.float32) - 0.2025 * moment.astype(jnp.float32)).astype(
        jnp.bfloat16
    )


def final_update(weight, stepped, moment, partner_share):
    updated = (
        0.05 * weight.astype(jnp.float32)
        + 0.475 * stepped.astype(jnp.float32)
        - 0.2025 * moment.astype(jnp.float32)
        + partner_share.astype(jnp.float32)
    )
    return updated.astype(jnp.bfloat16)


def body(w_gate, w_up, w_down, pool, rows_index, partners):
    weights = (w_gate[0], w_up[0], w_down[0])
    first, last = routes(partners)
    picked = jnp.take(pool[0], rows_index[0].reshape(-1), axis=0)
    picked = picked.reshape(ROUNDS, 2, -1, COLS)
    in_cols, out_cols = picked[:, 0], picked[:, 1]
    inputs = lax.all_gather(in_cols, TENSOR, axis=2, tiled=True)

    stepped = local_step(weights, inputs[0], in_cols[0], out_cols[0])
    theirs = partner_copy(first, stepped)
    results = [outer_update(*each) for each in zip(weights, stepped, theirs)]
    weights = tuple(r[0] for r in results)
    moments = tuple(r[1] for r in results)

    stepped = local_step(weights, inputs[1], in_cols[1], out_cols[1])
    shares = tuple(make_share(s, m) for s, m in zip(stepped, moments))
    theirs = partner_copy(last, shares)
    new = [final_update(*each) for each in zip(weights, stepped, moments, theirs)]
    return tuple(w[None] for w in new)


def solution(mesh):
    grid = Mesh(mesh.devices.reshape(4, 4, 4, 4, 2), ("x", "h", "y", "l", "c"))
    return jax.shard_map(
        body,
        mesh=grid,
        in_specs=(
            P(REPLICA, None, TENSOR),
            P(REPLICA, None, TENSOR),
            P(REPLICA, TENSOR, None),
            P(REPLICA, None, TENSOR),
            P(REPLICA, None, None, None),
            P(),
        ),
        out_specs=(
            P(REPLICA, None, TENSOR),
            P(REPLICA, None, TENSOR),
            P(REPLICA, TENSOR, None),
        ),
        check_vma=False,
    )
```

```python
import functools

import jax
import jax.numpy as jnp
from jax import lax
from jax.experimental import pallas as pl
from jax.experimental.pallas import tpu as pltpu
from jax.sharding import Mesh, PartitionSpec as P

D = 1024
FF = 3072
HID = 384
REPLICAS = 64
N_TENSOR = 8
COLS = D // N_TENSOR
PLANE = 16
PLANES = 4
ROUNDS = 2
IN_SCALE = D**-0.5
HID_SCALE = FF**-0.5

inner_rate = 1.0
outer_rate = 0.5
momentum_rate = 0.9

REPLICA = ("x", "h", "y")
FLAT = ("x", "y")
TENSOR = ("l", "c")

NEXT = 5
FAR = 4
VMEM = 48 << 20


def routes(partners):
    me = lax.axis_index("h")
    ids = jnp.arange(REPLICAS, dtype=jnp.int32)
    plane = (ids // 4) % PLANES
    flat = (ids // PLANE) * 4 + ids % 4
    to_plane = (partners // 4) % PLANES
    off = (to_plane - plane + PLANES) % PLANES
    same = (plane[:, None] == plane[None, :]) & (flat[None, :] < flat[:, None])
    rank = jnp.sum((same & (off[:, :, None] == off[:, None, :])).astype(jnp.int32), axis=2)
    places = jnp.arange(PLANE, dtype=jnp.int32)
    slots = places
    offs = jnp.array([1, 3, 2], jnp.int32)
    here = (plane == me)[None, None, None, :]
    sends = here & (off[:, None, None, :] == offs[None, :, None, None])
    sends = sends & (rank[:, None, None, :] == slots[None, None, :, None])
    send_index = jnp.sum(jnp.where(sends, flat, 0), axis=3)
    home = (places // 4) * PLANE + me * 4 + places % 4
    wanted = partners[:, None, :] == home[None, :, None]
    come_from = (plane[None, :] - me + PLANES) % PLANES
    kind = jnp.sum(jnp.where(wanted, come_from[:, None, :], 0), axis=2)
    place = jnp.where(off == 0, flat[None, :], rank)
    slot = jnp.sum(jnp.where(wanted, place[:, None, :], 0), axis=2)
    where = jnp.stack([kind, slot], axis=1)
    next_trips = jnp.max(jnp.where(off % 2 == 1, rank + 1 - NEXT, 0), axis=1)
    far_trips = jnp.max(jnp.where(off == 2, rank + 1 - FAR, 0), axis=1)
    return [(send_index[r], where[r], next_trips[r], far_trips[r]) for r in range(ROUNDS)]


def kernel_call(kernel, out_shape, index_args, args, name):
    scalars = [pl.BlockSpec(memory_space=pltpu.SMEM)] * len(index_args)
    whole = pl.BlockSpec(memory_space=pltpu.VMEM)
    size = sum(a.size * a.dtype.itemsize for a in (*args, *out_shape))
    return pl.pallas_call(
        kernel,
        out_shape=out_shape,
        in_specs=scalars + [whole] * len(args),
        out_specs=(whole,) * len(out_shape),
        compiler_params=pltpu.CompilerParams(vmem_limit_bytes=VMEM),
        cost_estimate=pl.CostEstimate(flops=size, bytes_accessed=size, transcendentals=0),
        name=name,
    )(*index_args, *args)


def pick_kernel(index, chunks, *outs):
    for o, out in enumerate(outs):

        @pl.loop(0, out.shape[0])
        def _(k, o=o, out=out):
            out[k] = chunks[index[o, k]]


def pick(index, chunks, counts):
    out_shape = tuple(jax.ShapeDtypeStruct((n, *chunks.shape[1:]), chunks.dtype) for n in counts)
    return kernel_call(pick_kernel, out_shape, (index,), (chunks,), "pick")


def merge_kernel(kinds, where, low, before, *refs):
    sources, out = refs[:-1], refs[-1]

    @pl.loop(0, PLANE)
    def _(d):
        kind, slot = where[0, d], where[1, d]
        out[d] = before[d]
        for i, (number, source) in enumerate(zip(kinds, sources)):
            at = slot - low[i]

            @pl.when((kind == number) & (at >= 0) & (at < source.shape[0]))
            def _(source=source, at=at):
                out[d] = source[at]


def merge(where, low, before, sources):
    kernel = functools.partial(merge_kernel, tuple(sources))
    out_shape = (jax.ShapeDtypeStruct(before.shape, before.dtype),)
    low = jnp.stack([jnp.int32(0) + low] * len(sources))
    return kernel_call(kernel, out_shape, (where, low), (before, *sources.values()), "merge")[0]


def step_by(n):
    return [(i, (i + n) % PLANES) for i in range(PLANES)]


def hop(sends):
    steps = {3: 1, 1: -1, 2: 2}
    return {k: lax.ppermute(s, "h", step_by(steps[k])) for k, s in sends.items()}


def depart(index, share):
    return dict(zip((3, 1, 2), pick(index, share, (NEXT, NEXT, FAR))))


def late(route, share, after):
    send_index, where, next_trips, far_trips = route
    start, _ = lax.optimization_barrier((jnp.int32(0), after))

    def next_one(state):
        i, placed = state
        at = NEXT + i
        index = lax.dynamic_slice(send_index, (0, at), (2, 1))
        came = hop(dict(zip((3, 1), pick(index, share, (1, 1)))))
        return i + 1, merge(where, at, placed, came)

    def far_one(state):
        i, placed = state
        at = FAR + i
        index = lax.dynamic_slice(send_index, (2, at), (1, 1))
        came = hop(dict(zip((2,), pick(index, share, (1,)))))
        return i + 1, merge(where, at, placed, came)

    _, placed = lax.while_loop(lambda s: s[0] < next_trips, next_one, (start, share))
    _, placed = lax.while_loop(lambda s: s[0] < far_trips, far_one, (start, placed))
    return placed


def over_plane(chunks):
    return lax.all_to_all(chunks, FLAT, 0, 0, tiled=True)


def swap(route, arrays):
    tie = lax.optimization_barrier
    shares, sent, came, done = [], [], [], []
    for a in arrays:
        a = a.reshape(PLANE, a.shape[0] // PLANE, a.shape[1])
        if shares:
            a, _ = tie((a, shares[-1]))
        shares.append(over_plane(a))
        sent.append(depart(route[0], shares[-1]))
        came.append(hop(sent[-1]))
    for i, share in enumerate(shares):
        placed = late(route, share, (sent[i], sent[min(i + 1, len(sent) - 1)]))
        parts, placed, _ = tie((came[i], placed, done))
        parts = {0: share, **parts}
        done = done + [over_plane(merge(route[1], 0, placed, parts))]
    return [d.reshape(a.shape) for d, a in zip(done, arrays)]


rows = (((0,), (0,)), ((), ()))


def grad(a, b):
    return lax.dot_general(a, b, rows, preferred_element_type=jnp.float32)


def local_step(weights, inputs, in_cols, out_cols):
    both, down = weights
    pre = jnp.dot(inputs, both, preferred_element_type=jnp.float32) * IN_SCALE
    gate_pre, up_value = pre[:, :HID], pre[:, HID:]
    sigmoid_gate = jax.nn.sigmoid(gate_pre)
    active = gate_pre * sigmoid_gate
    hidden = (active * up_value).astype(jnp.bfloat16)
    term = (
        lax.dot_general(hidden, down, (((1,), (1,)), ((), ())), preferred_element_type=jnp.float32)
        * HID_SCALE
    )
    blocks = term.astype(jnp.bfloat16).reshape(-1, N_TENSOR, COLS).transpose(1, 0, 2)
    terms = lax.all_to_all(blocks, TENSOR, 0, 0, tiled=True)
    branch = jnp.sum(terms.astype(jnp.float32), axis=0)
    error_cols = (in_cols.astype(jnp.float32) + branch - out_cols.astype(jnp.float32)).astype(
        jnp.bfloat16
    )
    errors = lax.all_gather(error_cols, TENSOR, axis=1, tiled=True)
    back = jnp.dot(errors, down, preferred_element_type=jnp.float32) * HID_SCALE
    delta_gate = back * up_value * sigmoid_gate * (1.0 + gate_pre * (1.0 - sigmoid_gate))
    delta_up = back * active
    deltas = jnp.concatenate([delta_gate, delta_up], axis=1).astype(jnp.bfloat16)
    gradients = (grad(inputs, deltas) * IN_SCALE, grad(errors, hidden) * HID_SCALE)
    return tuple(
        (w.astype(jnp.float32) - inner_rate * g).astype(jnp.bfloat16)
        for w, g in zip(weights, gradients)
    )


def partner_copy(route, arrays):
    return swap(route, arrays[::-1])[::-1]


def outer_update(weight, stepped, partner_step):
    weight = weight.astype(jnp.float32)
    pair_mean = 0.5 * (stepped.astype(jnp.float32) + partner_step.astype(jnp.float32))
    outer_grad = weight - pair_mean
    moment_new = outer_grad
    updated = weight - outer_rate * (momentum_rate * moment_new + outer_grad)
    return updated.astype(jnp.bfloat16), moment_new.astype(jnp.bfloat16)


def make_share(stepped, moment):
    return (0.475 * stepped.astype(jnp.float32) - 0.2025 * moment.astype(jnp.float32)).astype(
        jnp.bfloat16
    )


def final_update(weight, stepped, moment, partner_share):
    updated = (
        0.05 * weight.astype(jnp.float32)
        + 0.475 * stepped.astype(jnp.float32)
        - 0.2025 * moment.astype(jnp.float32)
        + partner_share.astype(jnp.float32)
    )
    return updated.astype(jnp.bfloat16)


def body(w_gate, w_up, w_down, pool, rows_index, partners):
    weights = (jnp.concatenate([w_gate[0], w_up[0]], axis=1), w_down[0].T)
    first, last = routes(partners)
    picked = jnp.take(pool[0], rows_index[0].reshape(-1), axis=0)
    picked = picked.reshape(ROUNDS, 2, -1, COLS)
    in_cols, out_cols = picked[:, 0], picked[:, 1]
    inputs = lax.all_gather(in_cols, TENSOR, axis=2, tiled=True)

    stepped = local_step(weights, inputs[0], in_cols[0], out_cols[0])
    theirs = partner_copy(first, stepped)
    results = [outer_update(*each) for each in zip(weights, stepped, theirs)]
    weights = tuple(r[0] for r in results)
    moments = tuple(r[1] for r in results)

    stepped = local_step(weights, inputs[1], in_cols[1], out_cols[1])
    shares = tuple(make_share(s, m) for s, m in zip(stepped, moments))
    theirs = partner_copy(last, shares)
    new = [final_update(*each) for each in zip(weights, stepped, moments, theirs)]
    both, down = new
    return both[None, :, :HID], both[None, :, HID:], down.T[None]


def solution(mesh):
    grid = Mesh(mesh.devices.reshape(4, 4, 4, 4, 2), ("x", "h", "y", "l", "c"))
    return jax.shard_map(
        body,
        mesh=grid,
        in_specs=(
            P(REPLICA, None, TENSOR),
            P(REPLICA, None, TENSOR),
            P(REPLICA, TENSOR, None),
            P(REPLICA, None, TENSOR),
            P(REPLICA, None, None, None),
            P(),
        ),
        out_specs=(
            P(REPLICA, None, TENSOR),
            P(REPLICA, None, TENSOR),
            P(REPLICA, TENSOR, None),
        ),
        check_vma=False,
    )
```

```python
import functools

import jax
import jax.numpy as jnp
from jax import lax
from jax.experimental import pallas as pl
from jax.experimental.pallas import tpu as pltpu
from jax.sharding import Mesh, PartitionSpec as P

D = 1024
FF = 3072
HID = 384
REPLICAS = 64
N_TENSOR = 8
COLS = D // N_TENSOR
PLANE = 16
PLANES = 4
ROUNDS = 2
IN_SCALE = D**-0.5
HID_SCALE = FF**-0.5

inner_rate = 1.0
outer_rate = 0.5
momentum_rate = 0.9

REPLICA = ("x", "h", "y")
FLAT = ("x", "y")
TENSOR = ("l", "c")

NEXT = 6
FAR = 5
VMEM = 48 << 20


def routes(partners):
    me = lax.axis_index("h")
    ids = jnp.arange(REPLICAS, dtype=jnp.int32)
    plane = (ids // 4) % PLANES
    flat = (ids // PLANE) * 4 + ids % 4
    to_plane = (partners // 4) % PLANES
    off = (to_plane - plane + PLANES) % PLANES
    same = (plane[:, None] == plane[None, :]) & (flat[None, :] < flat[:, None])
    rank = jnp.sum((same & (off[:, :, None] == off[:, None, :])).astype(jnp.int32), axis=2)
    places = jnp.arange(PLANE, dtype=jnp.int32)
    slots = places
    offs = jnp.array([1, 3, 2], jnp.int32)
    here = (plane == me)[None, None, None, :]
    sends = here & (off[:, None, None, :] == offs[None, :, None, None])
    sends = sends & (rank[:, None, None, :] == slots[None, None, :, None])
    send_index = jnp.sum(jnp.where(sends, flat, 0), axis=3)
    home = (places // 4) * PLANE + me * 4 + places % 4
    wanted = partners[:, None, :] == home[None, :, None]
    come_from = (plane[None, :] - me + PLANES) % PLANES
    kind = jnp.sum(jnp.where(wanted, come_from[:, None, :], 0), axis=2)
    place = jnp.where(off == 0, flat[None, :], rank)
    slot = jnp.sum(jnp.where(wanted, place[:, None, :], 0), axis=2)
    where = jnp.stack([kind, slot], axis=1)
    next_trips = jnp.max(jnp.where(off % 2 == 1, rank + 1 - NEXT, 0), axis=1)
    far_trips = jnp.max(jnp.where(off == 2, rank + 1 - FAR, 0), axis=1)
    return [(send_index[r], where[r], next_trips[r], far_trips[r]) for r in range(ROUNDS)]


def kernel_call(kernel, out_shape, index_args, args, name, outside=0, scratch=()):
    scalars = [pl.BlockSpec(memory_space=pltpu.SMEM)] * len(index_args)
    whole = pl.BlockSpec(memory_space=pltpu.VMEM)
    inside = [whole] * (len(args) - outside)
    size = sum(a.size * a.dtype.itemsize for a in (*args[: len(inside)], *out_shape))
    return pl.pallas_call(
        kernel,
        out_shape=out_shape,
        in_specs=scalars + inside + [pl.BlockSpec(memory_space=pl.ANY)] * outside,
        out_specs=(whole,) * len(out_shape),
        scratch_shapes=list(scratch),
        compiler_params=pltpu.CompilerParams(vmem_limit_bytes=VMEM),
        cost_estimate=pl.CostEstimate(flops=size, bytes_accessed=size, transcendentals=0),
        name=name,
    )(*index_args, *args)


def pick_kernel(index, chunks, *outs):
    for o, out in enumerate(outs):

        @pl.loop(0, out.shape[0])
        def _(k, o=o, out=out):
            out[k] = chunks[index[o, k]]


def pick(index, chunks, counts):
    out_shape = tuple(jax.ShapeDtypeStruct((n, *chunks.shape[1:]), chunks.dtype) for n in counts)
    return kernel_call(pick_kernel, out_shape, (index,), (chunks,), "pick")


def merge_kernel(kinds, column, where, *refs):
    n = len(kinds)
    sources, spare, out, sem = refs[:n], refs[n:-2], refs[-2], refs[-1]

    @pl.loop(0, PLANE)
    def _(d):
        kind, slot = where[0, d], where[1, d]
        for i, (number, source) in enumerate(zip(kinds, sources)):
            count = source.shape[0]

            @pl.when((kind == number) & (slot < count))
            def _(source=source):
                out[d] = source[slot]

            if number:

                @pl.when((kind == number) & (slot >= count))
                def _(source=spare[i - 1], count=count):
                    columns = pl.ds(column, out.shape[2])
                    copy = pltpu.make_async_copy(
                        source.at[slot - count, :, columns], out.at[d], sem
                    )
                    copy.start()
                    copy.wait()


def merge(where, sources, spare, column):
    share = sources[0]
    kernel = functools.partial(merge_kernel, tuple(sources), column)
    out_shape = (jax.ShapeDtypeStruct(share.shape, share.dtype),)
    args = (*sources.values(), *(spare[k] for k in sources if k))
    scratch = [pltpu.SemaphoreType.DMA]
    return kernel_call(kernel, out_shape, (where,), args, "merge", len(spare), scratch)[0]


def step_by(n):
    return [(i, (i + n) % PLANES) for i in range(PLANES)]


def hop(sends):
    steps = {3: 1, 1: -1, 2: 2}
    return {k: lax.ppermute(s, "h", step_by(steps[k])) for k, s in sends.items()}


def depart(index, share):
    return dict(zip((3, 1, 2), pick(index, share, (NEXT, NEXT, FAR))))


def pick_late_kernel(index, *refs):
    outs = refs[-index.shape[0] :]
    for o, out in enumerate(outs):
        at = 0
        for share in refs[: -len(outs)]:
            width = share.shape[2]
            out[0, :, at : at + width] = share[index[o, 0]]
            at += width


def late(route, shares, after):
    send_index, _, next_trips, far_trips = route
    start, _ = lax.optimization_barrier((jnp.int32(0), after))
    depth, width = shares[0].shape[1], sum(s.shape[2] for s in shares)

    def room(n):
        return jnp.zeros((PLANE - n, depth, width), shares[0].dtype)

    def trip(first, steps, slots):
        def one(state):
            i, came = state
            index = lax.dynamic_slice(send_index, (first, slots + i), (len(steps), 1))
            one_chunk = jax.ShapeDtypeStruct((1, depth, width), shares[0].dtype)
            sends = kernel_call(
                pick_late_kernel, (one_chunk,) * len(steps), (index,), shares, "pick"
            )
            new = hop(dict(zip(steps, sends)))
            return i + 1, {
                k: lax.dynamic_update_slice(old, new[k], (i, 0, 0)) for k, old in came.items()
            }

        return one

    _, near = lax.while_loop(
        lambda s: s[0] < next_trips,
        trip(0, (3, 1), NEXT),
        (start, {1: room(NEXT), 3: room(NEXT)}),
    )
    start, _ = lax.optimization_barrier((start, near))
    _, far = lax.while_loop(
        lambda s: s[0] < far_trips, trip(2, (2,), FAR), (start, {2: room(FAR)})
    )
    return {**near, **far}


def over_plane(chunks):
    return lax.all_to_all(chunks, FLAT, 0, 0, tiled=True)


def swap(route, arrays):
    tie = lax.optimization_barrier
    shares, sent, came, done = [], [], [], []
    for a in arrays:
        a = a.reshape(PLANE, a.shape[0] // PLANE, a.shape[1])
        if shares:
            a, _ = tie((a, shares[-1]))
        shares.append(over_plane(a))
        sent.append(depart(route[0], shares[-1]))
        came.append(hop(sent[-1]))
    spare, column, placed = late(route, shares, (sent, came[0])), 0, []
    for share, parts in zip(shares, came):
        parts, spare = tie((parts, spare))
        placed.append(merge(route[1], {0: share, **parts}, spare, column))
        column += share.shape[2]
    placed[0], _ = tie((placed[0], came))
    done = [over_plane(p) for p in placed]
    return [d.reshape(a.shape) for d, a in zip(done, arrays)]


rows = (((0,), (0,)), ((), ()))


def grad(a, b):
    return lax.dot_general(a, b, rows, preferred_element_type=jnp.float32)


def local_step(weights, inputs, in_cols, out_cols):
    both, down = weights
    pre = jnp.dot(inputs, both, preferred_element_type=jnp.float32) * IN_SCALE
    gate_pre, up_value = pre[:, :HID], pre[:, HID:]
    sigmoid_gate = jax.nn.sigmoid(gate_pre)
    active = gate_pre * sigmoid_gate
    hidden = (active * up_value).astype(jnp.bfloat16)
    term = (
        lax.dot_general(hidden, down, (((1,), (1,)), ((), ())), preferred_element_type=jnp.float32)
        * HID_SCALE
    )
    blocks = term.astype(jnp.bfloat16).reshape(-1, N_TENSOR, COLS).transpose(1, 0, 2)
    terms = lax.all_to_all(blocks, TENSOR, 0, 0, tiled=True)
    branch = jnp.sum(terms.astype(jnp.float32), axis=0)
    error_cols = (in_cols.astype(jnp.float32) + branch - out_cols.astype(jnp.float32)).astype(
        jnp.bfloat16
    )
    errors = lax.all_gather(error_cols, TENSOR, axis=1, tiled=True)
    back = jnp.dot(errors, down, preferred_element_type=jnp.float32) * HID_SCALE
    delta_gate = back * up_value * sigmoid_gate * (1.0 + gate_pre * (1.0 - sigmoid_gate))
    delta_up = back * active
    deltas = jnp.concatenate([delta_gate, delta_up], axis=1).astype(jnp.bfloat16)
    gradients = (grad(inputs, deltas) * IN_SCALE, grad(errors, hidden) * HID_SCALE)
    return tuple(
        (w.astype(jnp.float32) - inner_rate * g).astype(jnp.bfloat16)
        for w, g in zip(weights, gradients)
    )


def partner_copy(route, arrays):
    return swap(route, arrays[::-1])[::-1]


def outer_update(weight, stepped, partner_step):
    weight = weight.astype(jnp.float32)
    pair_mean = 0.5 * (stepped.astype(jnp.float32) + partner_step.astype(jnp.float32))
    outer_grad = weight - pair_mean
    moment_new = outer_grad
    updated = weight - outer_rate * (momentum_rate * moment_new + outer_grad)
    return updated.astype(jnp.bfloat16), moment_new.astype(jnp.bfloat16)


def make_share(stepped, moment):
    return (0.475 * stepped.astype(jnp.float32) - 0.2025 * moment.astype(jnp.float32)).astype(
        jnp.bfloat16
    )


def final_update(weight, stepped, moment, partner_share):
    updated = (
        0.05 * weight.astype(jnp.float32)
        + 0.475 * stepped.astype(jnp.float32)
        - 0.2025 * moment.astype(jnp.float32)
        + partner_share.astype(jnp.float32)
    )
    return updated.astype(jnp.bfloat16)


def body(w_gate, w_up, w_down, pool, rows_index, partners):
    weights = (jnp.concatenate([w_gate[0], w_up[0]], axis=1), w_down[0].T)
    first, last = routes(partners)
    picked = jnp.take(pool[0], rows_index[0].reshape(-1), axis=0)
    picked = picked.reshape(ROUNDS, 2, -1, COLS)
    in_cols, out_cols = picked[:, 0], picked[:, 1]
    inputs = lax.all_gather(in_cols, TENSOR, axis=2, tiled=True)

    stepped = local_step(weights, inputs[0], in_cols[0], out_cols[0])
    theirs = partner_copy(first, stepped)
    results = [outer_update(*each) for each in zip(weights, stepped, theirs)]
    weights = tuple(r[0] for r in results)
    moments = tuple(r[1] for r in results)

    stepped = local_step(weights, inputs[1], in_cols[1], out_cols[1])
    shares = tuple(make_share(s, m) for s, m in zip(stepped, moments))
    theirs = partner_copy(last, shares)
    new = [final_update(*each) for each in zip(weights, stepped, moments, theirs)]
    both, down = new
    return both[None, :, :HID], both[None, :, HID:], down.T[None]


def solution(mesh):
    grid = Mesh(mesh.devices.reshape(4, 4, 4, 4, 2), ("x", "h", "y", "l", "c"))
    return jax.shard_map(
        body,
        mesh=grid,
        in_specs=(
            P(REPLICA, None, TENSOR),
            P(REPLICA, None, TENSOR),
            P(REPLICA, TENSOR, None),
            P(REPLICA, None, TENSOR),
            P(REPLICA, None, None, None),
            P(),
        ),
        out_specs=(
            P(REPLICA, None, TENSOR),
            P(REPLICA, None, TENSOR),
            P(REPLICA, TENSOR, None),
        ),
        check_vma=False,
    )
```

```python
import functools

import jax
import jax.numpy as jnp
from jax import lax
from jax.experimental import pallas as pl
from jax.experimental.pallas import tpu as pltpu
from jax.sharding import Mesh, PartitionSpec as P

D = 1024
FF = 3072
HID = 384
REPLICAS = 64
N_TENSOR = 8
COLS = D // N_TENSOR
PLANE = 16
PLANES = 4
ROUNDS = 2
IN_SCALE = D**-0.5
HID_SCALE = FF**-0.5

inner_rate = 1.0
outer_rate = 0.5
momentum_rate = 0.9

REPLICA = ("x", "h", "y")
FLAT = ("x", "y")
TENSOR = ("l", "c")

NEXT = 6
FAR = 5
VMEM = 48 << 20


def routes(partners):
    me = lax.axis_index("h")
    ids = jnp.arange(REPLICAS, dtype=jnp.int32)
    plane = (ids // 4) % PLANES
    flat = (ids // PLANE) * 4 + ids % 4
    to_plane = (partners // 4) % PLANES
    off = (to_plane - plane + PLANES) % PLANES
    same = (plane[:, None] == plane[None, :]) & (flat[None, :] < flat[:, None])
    rank = jnp.sum((same & (off[:, :, None] == off[:, None, :])).astype(jnp.int32), axis=2)
    places = jnp.arange(PLANE, dtype=jnp.int32)
    slots = places
    offs = jnp.array([1, 3, 2], jnp.int32)
    here = (plane == me)[None, None, None, :]
    sends = here & (off[:, None, None, :] == offs[None, :, None, None])
    sends = sends & (rank[:, None, None, :] == slots[None, None, :, None])
    send_index = jnp.sum(jnp.where(sends, flat, 0), axis=3)
    home = (places // 4) * PLANE + me * 4 + places % 4
    wanted = partners[:, None, :] == home[None, :, None]
    come_from = (plane[None, :] - me + PLANES) % PLANES
    kind = jnp.sum(jnp.where(wanted, come_from[:, None, :], 0), axis=2)
    place = jnp.where(off == 0, flat[None, :], rank)
    slot = jnp.sum(jnp.where(wanted, place[:, None, :], 0), axis=2)
    where = jnp.stack([kind, slot], axis=1)
    next_trips = jnp.max(jnp.where(off % 2 == 1, rank + 1 - NEXT, 0), axis=1)
    far_trips = jnp.max(jnp.where(off == 2, rank + 1 - FAR, 0), axis=1)
    return [(send_index[r], where[r], next_trips[r], far_trips[r]) for r in range(ROUNDS)]


def kernel_call(kernel, out_shape, index_args, args, name, outside=0, scratch=()):
    scalars = [pl.BlockSpec(memory_space=pltpu.SMEM)] * len(index_args)
    whole = pl.BlockSpec(memory_space=pltpu.VMEM)
    inside = [whole] * (len(args) - outside)
    size = sum(a.size * a.dtype.itemsize for a in (*args[: len(inside)], *out_shape))
    return pl.pallas_call(
        kernel,
        out_shape=out_shape,
        in_specs=scalars + inside + [pl.BlockSpec(memory_space=pl.ANY)] * outside,
        out_specs=(whole,) * len(out_shape),
        scratch_shapes=list(scratch),
        compiler_params=pltpu.CompilerParams(vmem_limit_bytes=VMEM),
        cost_estimate=pl.CostEstimate(flops=size, bytes_accessed=size, transcendentals=0),
        name=name,
    )(*index_args, *args)


def pick_kernel(index, *refs):
    outs = refs[-index.shape[0] :]
    for o, out in enumerate(outs):

        @pl.loop(0, out.shape[0])
        def _(k, o=o, out=out):
            at = 0
            for share in refs[: -len(outs)]:
                width = share.shape[2]
                out[k, :, at : at + width] = share[index[o, k]]
                at += width


def pick(index, shares, counts):
    depth, width = shares[0].shape[1], sum(s.shape[2] for s in shares)
    out_shape = tuple(jax.ShapeDtypeStruct((n, depth, width), shares[0].dtype) for n in counts)
    return kernel_call(pick_kernel, out_shape, (index,), shares, "pick")


def merge_kernel(layout, where, *refs):
    out, sem = refs[-2:]
    spare = dict(zip((1, 3, 2), refs[-5:-2]))

    @pl.loop(0, PLANE)
    def _(d):
        kind, slot = where[0, d], where[1, d]
        for (number, column), source in zip(layout, refs):
            count, _, width = source.shape

            @pl.when((kind == number) & (slot < count))
            def _(source=source, column=column, width=width):
                out[d, :, column : column + width] = source[slot]

        for number, source in spare.items():
            count = PLANE - source.shape[0]

            @pl.when((kind == number) & (slot >= count))
            def _(source=source, count=count):
                copy = pltpu.make_async_copy(source.at[slot - count], out.at[d], sem)
                copy.start()
                copy.wait()


def merge(where, sources, spare):
    layout = tuple((number, column) for number, column, _ in sources)
    chunks = [c for _, _, c in sources]
    _, depth, width = spare[1].shape
    out_shape = (jax.ShapeDtypeStruct((PLANE, depth, width), chunks[0].dtype),)
    args = (*chunks, spare[1], spare[3], spare[2])
    scratch = [pltpu.SemaphoreType.DMA]
    kernel = functools.partial(merge_kernel, layout)
    return kernel_call(kernel, out_shape, (where,), args, "merge", len(spare), scratch)[0]


def room(n, like):
    return pl.pallas_call(
        lambda out: None,
        out_shape=jax.ShapeDtypeStruct((PLANE - n, *like), jnp.bfloat16),
        out_specs=pl.BlockSpec(memory_space=pl.ANY),
        name="room",
    )()


def step_by(n):
    return [(i, (i + n) % PLANES) for i in range(PLANES)]


def hop(sends):
    steps = {3: 1, 1: -1, 2: 2}
    return {k: lax.ppermute(s, "h", step_by(steps[k])) for k, s in sends.items()}


def late(route, shares, after):
    send_index, _, next_trips, far_trips = route
    start, _ = lax.optimization_barrier((jnp.int32(0), after))
    like = (shares[0].shape[1], sum(s.shape[2] for s in shares))

    def trip(first, steps, slots):
        def one(state):
            i, came = state
            index = lax.dynamic_slice(send_index, (first, slots + i), (len(steps), 1))
            new = hop(dict(zip(steps, pick(index, shares, (1,) * len(steps)))))
            return i + 1, {
                k: lax.dynamic_update_slice(old, new[k], (i, 0, 0)) for k, old in came.items()
            }

        return one

    _, near = lax.while_loop(
        lambda s: s[0] < next_trips,
        trip(0, (3, 1), NEXT),
        (start, {1: room(NEXT, like), 3: room(NEXT, like)}),
    )
    start, _ = lax.optimization_barrier((start, near))
    _, far = lax.while_loop(
        lambda s: s[0] < far_trips, trip(2, (2,), FAR), (start, {2: room(FAR, like)})
    )
    return {**near, **far}


def over_plane(chunks):
    return lax.all_to_all(chunks, FLAT, 0, 0, tiled=True)


def swap(route, arrays):
    tie = lax.optimization_barrier
    send_index, where = route[:2]
    shares, sources, sent, column = [], [], [], 0
    for a in arrays:
        a = a.reshape(PLANE, a.shape[0] // PLANE, a.shape[1])
        if shares:
            a, _ = tie((a, shares[-1]))
        share = over_plane(a)
        sent.append(pick(send_index[:2], (share,), (NEXT, NEXT)))
        came = hop(dict(zip((3, 1), sent[-1])))
        shares.append(share)
        sources += [(number, column, chunks) for number, chunks in {0: share, **came}.items()]
        column += share.shape[2]
    sent.append(pick(send_index[2:], shares, (FAR,)))
    far = hop({2: sent[-1][0]})
    spare = late(route, shares, (sent, [chunks for _, _, chunks in sources[:3]]))
    sources.append((2, 0, far[2]))
    placed = over_plane(merge(where, sources, spare)).reshape(-1, column)
    at = [sum(a.shape[1] for a in arrays[:i]) for i in range(len(arrays))]
    return [placed[:, i : i + a.shape[1]] for i, a in zip(at, arrays)]


rows = (((0,), (0,)), ((), ()))


def grad(a, b):
    return lax.dot_general(a, b, rows, preferred_element_type=jnp.float32)


def local_step(weights, inputs, in_cols, out_cols):
    both, down = weights
    pre = jnp.dot(inputs, both, preferred_element_type=jnp.float32) * IN_SCALE
    gate_pre, up_value = pre[:, :HID], pre[:, HID:]
    sigmoid_gate = jax.nn.sigmoid(gate_pre)
    active = gate_pre * sigmoid_gate
    hidden = (active * up_value).astype(jnp.bfloat16)
    term = (
        lax.dot_general(hidden, down, (((1,), (1,)), ((), ())), preferred_element_type=jnp.float32)
        * HID_SCALE
    )
    blocks = term.astype(jnp.bfloat16).reshape(-1, N_TENSOR, COLS).transpose(1, 0, 2)
    terms = lax.all_to_all(blocks, TENSOR, 0, 0, tiled=True)
    branch = jnp.sum(terms.astype(jnp.float32), axis=0)
    error_cols = (in_cols.astype(jnp.float32) + branch - out_cols.astype(jnp.float32)).astype(
        jnp.bfloat16
    )
    errors = lax.all_gather(error_cols, TENSOR, axis=1, tiled=True)
    back = jnp.dot(errors, down, preferred_element_type=jnp.float32) * HID_SCALE
    delta_gate = back * up_value * sigmoid_gate * (1.0 + gate_pre * (1.0 - sigmoid_gate))
    delta_up = back * active
    deltas = jnp.concatenate([delta_gate, delta_up], axis=1).astype(jnp.bfloat16)
    gradients = (grad(inputs, deltas) * IN_SCALE, grad(errors, hidden) * HID_SCALE)
    return tuple(
        (w.astype(jnp.float32) - inner_rate * g).astype(jnp.bfloat16)
        for w, g in zip(weights, gradients)
    )


def partner_copy(route, arrays):
    return swap(route, arrays[::-1])[::-1]


def outer_update(weight, stepped, partner_step):
    weight = weight.astype(jnp.float32)
    pair_mean = 0.5 * (stepped.astype(jnp.float32) + partner_step.astype(jnp.float32))
    outer_grad = weight - pair_mean
    moment_new = outer_grad
    updated = weight - outer_rate * (momentum_rate * moment_new + outer_grad)
    return updated.astype(jnp.bfloat16), moment_new.astype(jnp.bfloat16)


def make_share(stepped, moment):
    return (0.475 * stepped.astype(jnp.float32) - 0.2025 * moment.astype(jnp.float32)).astype(
        jnp.bfloat16
    )


def final_update(weight, stepped, moment, partner_share):
    updated = (
        0.05 * weight.astype(jnp.float32)
        + 0.475 * stepped.astype(jnp.float32)
        - 0.2025 * moment.astype(jnp.float32)
        + partner_share.astype(jnp.float32)
    )
    return updated.astype(jnp.bfloat16)


def body(w_gate, w_up, w_down, pool, rows_index, partners):
    weights = (jnp.concatenate([w_gate[0], w_up[0]], axis=1), w_down[0].T)
    first, last = routes(partners)
    picked = jnp.take(pool[0], rows_index[0].reshape(-1), axis=0)
    picked = picked.reshape(ROUNDS, 2, -1, COLS)
    in_cols, out_cols = picked[:, 0], picked[:, 1]
    inputs = lax.all_gather(in_cols, TENSOR, axis=2, tiled=True)

    stepped = local_step(weights, inputs[0], in_cols[0], out_cols[0])
    theirs = partner_copy(first, stepped)
    results = [outer_update(*each) for each in zip(weights, stepped, theirs)]
    weights = tuple(r[0] for r in results)
    moments = tuple(r[1] for r in results)

    stepped = local_step(weights, inputs[1], in_cols[1], out_cols[1])
    shares = tuple(make_share(s, m) for s, m in zip(stepped, moments))
    theirs = partner_copy(last, shares)
    new = [final_update(*each) for each in zip(weights, stepped, moments, theirs)]
    both, down = new
    return both[None, :, :HID], both[None, :, HID:], down.T[None]


def solution(mesh):
    grid = Mesh(mesh.devices.reshape(4, 4, 4, 4, 2), ("x", "h", "y", "l", "c"))
    return jax.shard_map(
        body,
        mesh=grid,
        in_specs=(
            P(REPLICA, None, TENSOR),
            P(REPLICA, None, TENSOR),
            P(REPLICA, TENSOR, None),
            P(REPLICA, None, TENSOR),
            P(REPLICA, None, None, None),
            P(),
        ),
        out_specs=(
            P(REPLICA, None, TENSOR),
            P(REPLICA, None, TENSOR),
            P(REPLICA, TENSOR, None),
        ),
        check_vma=False,
    )
```

```python
import functools

import jax
import jax.numpy as jnp
from jax import lax
from jax.experimental import pallas as pl
from jax.experimental.pallas import tpu as pltpu
from jax.sharding import Mesh, PartitionSpec as P

D = 1024
FF = 3072
HID = 384
REPLICAS = 64
N_TENSOR = 8
COLS = D // N_TENSOR
PLANE = 16
PLANES = 4
ROUNDS = 2
IN_SCALE = D**-0.5
HID_SCALE = FF**-0.5

inner_rate = 1.0
outer_rate = 0.5
momentum_rate = 0.9

REPLICA = ("x", "h", "y")
FLAT = ("x", "y")
TENSOR = ("l", "c")

NEXT = 6
FAR = 5
VMEM = 48 << 20


def routes(partners):
    me = lax.axis_index("h")
    ids = jnp.arange(REPLICAS, dtype=jnp.int32)
    plane = (ids // 4) % PLANES
    flat = (ids // PLANE) * 4 + ids % 4
    to_plane = (partners // 4) % PLANES
    off = (to_plane - plane + PLANES) % PLANES
    same = (plane[:, None] == plane[None, :]) & (flat[None, :] < flat[:, None])
    rank = jnp.sum((same & (off[:, :, None] == off[:, None, :])).astype(jnp.int32), axis=2)
    places = jnp.arange(PLANE, dtype=jnp.int32)
    slots = places
    offs = jnp.array([1, 3, 2], jnp.int32)
    here = (plane == me)[None, None, None, :]
    sends = here & (off[:, None, None, :] == offs[None, :, None, None])
    sends = sends & (rank[:, None, None, :] == slots[None, None, :, None])
    send_index = jnp.sum(jnp.where(sends, flat, 0), axis=3)
    home = (places // 4) * PLANE + me * 4 + places % 4
    wanted = partners[:, None, :] == home[None, :, None]
    come_from = (plane[None, :] - me + PLANES) % PLANES
    kind = jnp.sum(jnp.where(wanted, come_from[:, None, :], 0), axis=2)
    place = jnp.where(off == 0, flat[None, :], rank)
    slot = jnp.sum(jnp.where(wanted, place[:, None, :], 0), axis=2)
    where = jnp.stack([kind, slot], axis=1)
    next_trips = jnp.max(jnp.where(off % 2 == 1, rank + 1 - NEXT, 0), axis=1)
    far_trips = jnp.max(jnp.where(off == 2, rank + 1 - FAR, 0), axis=1)
    return [(send_index[r], where[r], next_trips[r], far_trips[r]) for r in range(ROUNDS)]


def kernel_call(kernel, out_shape, index_args, args, name, outside=0, scratch=()):
    scalars = [pl.BlockSpec(memory_space=pltpu.SMEM)] * len(index_args)
    whole = pl.BlockSpec(memory_space=pltpu.VMEM)
    inside = [whole] * (len(args) - outside)
    size = sum(a.size * a.dtype.itemsize for a in (*args[: len(inside)], *out_shape))
    return pl.pallas_call(
        kernel,
        out_shape=out_shape,
        in_specs=scalars + inside + [pl.BlockSpec(memory_space=pl.ANY)] * outside,
        out_specs=(whole,) * len(out_shape),
        scratch_shapes=list(scratch),
        compiler_params=pltpu.CompilerParams(vmem_limit_bytes=VMEM),
        cost_estimate=pl.CostEstimate(flops=size, bytes_accessed=size, transcendentals=0),
        name=name,
    )(*index_args, *args)


def pick_kernel(index, *refs):
    outs = refs[-index.shape[0] :]
    for o, out in enumerate(outs):

        @pl.loop(0, out.shape[0])
        def _(k, o=o, out=out):
            at = 0
            for share in refs[: -len(outs)]:
                width = share.shape[2]
                out[k, :, at : at + width] = share[index[o, k]]
                at += width


def pick(index, shares, counts):
    depth, width = shares[0].shape[1], sum(s.shape[2] for s in shares)
    out_shape = tuple(jax.ShapeDtypeStruct((n, depth, width), shares[0].dtype) for n in counts)
    return kernel_call(pick_kernel, out_shape, (index,), shares, "pick")


def merge_kernel(layout, where, *refs):
    out, sem = refs[-2:]
    spare = dict(zip((1, 3, 2), refs[-5:-2]))

    @pl.loop(0, PLANE)
    def _(d):
        kind, slot = where[0, d], where[1, d]
        for (number, column), source in zip(layout, refs):
            count, _, width = source.shape

            @pl.when((kind == number) & (slot < count))
            def _(source=source, column=column, width=width):
                out[d, :, column : column + width] = source[slot]

        for number, source in spare.items():
            count = PLANE - source.shape[0]

            @pl.when((kind == number) & (slot >= count))
            def _(source=source, count=count):
                copy = pltpu.make_async_copy(source.at[slot - count], out.at[d], sem)
                copy.start()
                copy.wait()


def merge(where, sources, spare):
    layout = tuple((number, column) for number, column, _ in sources)
    chunks = [c for _, _, c in sources]
    _, depth, width = spare[1].shape
    out_shape = (jax.ShapeDtypeStruct((PLANE, depth, width), chunks[0].dtype),)
    args = (*chunks, spare[1], spare[3], spare[2])
    scratch = [pltpu.SemaphoreType.DMA]
    kernel = functools.partial(merge_kernel, layout)
    return kernel_call(kernel, out_shape, (where,), args, "merge", len(spare), scratch)[0]


def room(n, like):
    return pl.pallas_call(
        lambda out: None,
        out_shape=jax.ShapeDtypeStruct((PLANE - n, *like), jnp.bfloat16),
        out_specs=pl.BlockSpec(memory_space=pl.ANY),
        name="room",
    )()


def step_by(n):
    return [(i, (i + n) % PLANES) for i in range(PLANES)]


def hop(sends):
    steps = {3: 1, 1: -1, 2: 2}
    return {k: lax.ppermute(s, "h", step_by(steps[k])) for k, s in sends.items()}


def late(route, shares, after):
    send_index, _, next_trips, far_trips = route
    start, _ = lax.optimization_barrier((jnp.int32(0), after))
    like = (shares[0].shape[1], sum(s.shape[2] for s in shares))

    def trip(first, steps, slots):
        def one(state):
            i, came = state
            index = lax.dynamic_slice(send_index, (first, slots + i), (len(steps), 1))
            new = hop(dict(zip(steps, pick(index, shares, (1,) * len(steps)))))
            return i + 1, {
                k: lax.dynamic_update_slice(old, new[k], (i, 0, 0)) for k, old in came.items()
            }

        return one

    _, near = lax.while_loop(
        lambda s: s[0] < next_trips,
        trip(0, (3, 1), NEXT),
        (start, {1: room(NEXT, like), 3: room(NEXT, like)}),
    )
    start, _ = lax.optimization_barrier((start, near))
    _, far = lax.while_loop(
        lambda s: s[0] < far_trips, trip(2, (2,), FAR), (start, {2: room(FAR, like)})
    )
    return {**near, **far}


def over_plane(chunks):
    return lax.all_to_all(chunks, FLAT, 0, 0, tiled=True)


def swap(route, arrays):
    tie = lax.optimization_barrier
    send_index, where = route[:2]
    shares, sources, sent, column = [], [], [], 0
    for a in arrays:
        a = a.reshape(PLANE, a.shape[0] // PLANE, a.shape[1])
        if shares:
            a, _ = tie((a, shares[-1]))
        share = over_plane(a)
        sent.append(pick(send_index[:2], (share,), (NEXT, NEXT)))
        came = hop(dict(zip((3, 1), sent[-1])))
        shares.append(share)
        sources += [(number, column, chunks) for number, chunks in {0: share, **came}.items()]
        column += share.shape[2]
    sent.append(pick(send_index[2:], shares, (FAR,)))
    far = hop({2: sent[-1][0]})
    spare = late(route, shares, (sent, [chunks for _, _, chunks in sources[:3]]))
    sources.append((2, 0, far[2]))
    placed = over_plane(merge(where, sources, spare)).reshape(-1, column)
    at = [sum(a.shape[1] for a in arrays[:i]) for i in range(len(arrays))]
    return [placed[:, i : i + a.shape[1]] for i, a in zip(at, arrays)]


rows = (((0,), (0,)), ((), ()))


def grad(a, b):
    return lax.dot_general(a, b, rows, preferred_element_type=jnp.float32)


def local_step(weights, inputs, in_cols, out_cols):
    both, down = weights
    pre = jnp.dot(inputs, both, preferred_element_type=jnp.float32) * IN_SCALE
    gate_pre, up_value = pre[:, :HID], pre[:, HID:]
    sigmoid_gate = jax.nn.sigmoid(gate_pre)
    active = gate_pre * sigmoid_gate
    hidden = (active * up_value).astype(jnp.bfloat16)
    term = (
        lax.dot_general(hidden, down, (((1,), (1,)), ((), ())), preferred_element_type=jnp.float32)
        * HID_SCALE
    )
    blocks = term.astype(jnp.bfloat16).reshape(-1, N_TENSOR, COLS).transpose(1, 0, 2)
    terms = lax.all_to_all(blocks, TENSOR, 0, 0, tiled=True)
    branch = jnp.sum(terms.astype(jnp.float32), axis=0)
    error_cols = (in_cols.astype(jnp.float32) + branch - out_cols.astype(jnp.float32)).astype(
        jnp.bfloat16
    )
    errors = lax.all_gather(error_cols, TENSOR, axis=1, tiled=True)
    back = jnp.dot(errors, down, preferred_element_type=jnp.float32) * HID_SCALE
    delta_gate = back * up_value * sigmoid_gate * (1.0 + gate_pre * (1.0 - sigmoid_gate))
    delta_up = back * active
    deltas = jnp.concatenate([delta_gate, delta_up], axis=1).astype(jnp.bfloat16)
    gradients = (grad(inputs, deltas) * IN_SCALE, grad(errors, hidden) * HID_SCALE)
    return tuple(
        (w.astype(jnp.float32) - inner_rate * g).astype(jnp.bfloat16)
        for w, g in zip(weights, gradients)
    )


def partner_copy(route, arrays):
    return swap(route, arrays[::-1])[::-1]


def outer_update(weight, stepped, partner_step):
    weight = weight.astype(jnp.float32)
    pair_mean = 0.5 * (stepped.astype(jnp.float32) + partner_step.astype(jnp.float32))
    outer_grad = weight - pair_mean
    moment_new = outer_grad
    updated = weight - outer_rate * (momentum_rate * moment_new + outer_grad)
    return updated.astype(jnp.bfloat16), moment_new.astype(jnp.bfloat16)


def make_share(stepped, moment):
    return (0.475 * stepped.astype(jnp.float32) - 0.2025 * moment.astype(jnp.float32)).astype(
        jnp.bfloat16
    )


def final_update(weight, stepped, moment, partner_share):
    updated = (
        0.05 * weight.astype(jnp.float32)
        + 0.475 * stepped.astype(jnp.float32)
        - 0.2025 * moment.astype(jnp.float32)
        + partner_share.astype(jnp.float32)
    )
    return updated.astype(jnp.bfloat16)


def body(w_gate, w_up, w_down, pool, rows_index, partners):
    weights = (jnp.concatenate([w_gate[0], w_up[0]], axis=1), w_down[0].T)
    first, last = routes(partners)
    picked = jnp.take(pool[0], rows_index[0].reshape(-1), axis=0)
    picked = picked.reshape(ROUNDS, 2, -1, COLS)
    in_cols, out_cols = picked[:, 0], picked[:, 1]
    inputs = lax.all_gather(in_cols, TENSOR, axis=2, tiled=True)

    stepped = local_step(weights, inputs[0], in_cols[0], out_cols[0])
    theirs = partner_copy(first, stepped)
    results = [outer_update(*each) for each in zip(weights, stepped, theirs)]
    weights = tuple(r[0] for r in results)
    moments = tuple(r[1] for r in results)

    stepped = local_step(weights, inputs[1], in_cols[1], out_cols[1])
    shares = tuple(make_share(s, m) for s, m in zip(stepped, moments))
    theirs = partner_copy(last, shares)
    both, down = zip(weights, stepped, moments, theirs)
    gate = final_update(*(a[:, :HID] for a in both))
    up = final_update(*(a[:, HID:] for a in both))
    return gate[None], up[None], final_update(*(a.T for a in down))[None]


def solution(mesh):
    grid = Mesh(mesh.devices.reshape(4, 4, 4, 4, 2), ("x", "h", "y", "l", "c"))
    return jax.shard_map(
        body,
        mesh=grid,
        in_specs=(
            P(REPLICA, None, TENSOR),
            P(REPLICA, None, TENSOR),
            P(REPLICA, TENSOR, None),
            P(REPLICA, None, TENSOR),
            P(REPLICA, None, None, None),
            P(),
        ),
        out_specs=(
            P(REPLICA, None, TENSOR),
            P(REPLICA, None, TENSOR),
            P(REPLICA, TENSOR, None),
        ),
        check_vma=False,
    )
```

```python
import functools

import jax
import jax.numpy as jnp
from jax import lax
from jax.experimental import pallas as pl
from jax.experimental.pallas import tpu as pltpu
from jax.sharding import Mesh, PartitionSpec as P

D = 1024
FF = 3072
HID = 384
REPLICAS = 64
N_TENSOR = 8
COLS = D // N_TENSOR
PLANE = 16
PLANES = 4
ROUNDS = 2
IN_SCALE = D**-0.5
HID_SCALE = FF**-0.5

inner_rate = 1.0
outer_rate = 0.5
momentum_rate = 0.9

REPLICA = ("x", "h", "y")
FLAT = ("x", "y")
TENSOR = ("l", "c")

NEXT = 6
FAR = 5
VMEM = 48 << 20


def routes(partners):
    me = lax.axis_index("h")
    ids = jnp.arange(REPLICAS, dtype=jnp.int32)
    plane = (ids // 4) % PLANES
    flat = (ids // PLANE) * 4 + ids % 4
    to_plane = (partners // 4) % PLANES
    off = (to_plane - plane + PLANES) % PLANES
    same = (plane[:, None] == plane[None, :]) & (flat[None, :] < flat[:, None])
    rank = jnp.sum((same & (off[:, :, None] == off[:, None, :])).astype(jnp.int32), axis=2)
    places = jnp.arange(PLANE, dtype=jnp.int32)
    slots = places
    offs = jnp.array([1, 3, 2], jnp.int32)
    here = (plane == me)[None, None, None, :]
    sends = here & (off[:, None, None, :] == offs[None, :, None, None])
    sends = sends & (rank[:, None, None, :] == slots[None, None, :, None])
    send_index = jnp.sum(jnp.where(sends, flat, 0), axis=3)
    home = (places // 4) * PLANE + me * 4 + places % 4
    wanted = partners[:, None, :] == home[None, :, None]
    come_from = (plane[None, :] - me + PLANES) % PLANES
    kind = jnp.sum(jnp.where(wanted, come_from[:, None, :], 0), axis=2)
    place = jnp.where(off == 0, flat[None, :], rank)
    slot = jnp.sum(jnp.where(wanted, place[:, None, :], 0), axis=2)
    where = jnp.stack([kind, slot], axis=1)
    next_trips = jnp.max(jnp.where(off % 2 == 1, rank + 1 - NEXT, 0), axis=1)
    far_trips = jnp.max(jnp.where(off == 2, rank + 1 - FAR, 0), axis=1)
    return [(send_index[r], where[r], next_trips[r], far_trips[r]) for r in range(ROUNDS)]


def kernel_call(kernel, out_shape, index_args, args, name, outside=0, scratch=()):
    scalars = [pl.BlockSpec(memory_space=pltpu.SMEM)] * len(index_args)
    whole = pl.BlockSpec(memory_space=pltpu.VMEM)
    inside = [whole] * (len(args) - outside)
    size = sum(a.size * a.dtype.itemsize for a in (*args[: len(inside)], *out_shape))
    return pl.pallas_call(
        kernel,
        out_shape=out_shape,
        in_specs=scalars + inside + [pl.BlockSpec(memory_space=pl.ANY)] * outside,
        out_specs=(whole,) * len(out_shape),
        scratch_shapes=list(scratch),
        compiler_params=pltpu.CompilerParams(vmem_limit_bytes=VMEM),
        cost_estimate=pl.CostEstimate(flops=size, bytes_accessed=size, transcendentals=0),
        name=name,
    )(*index_args, *args)


def pick_kernel(index, chunks, *outs):
    for o, out in enumerate(outs):

        @pl.loop(0, out.shape[0])
        def _(k, o=o, out=out):
            out[k] = chunks[index[o, k]]


def pick(index, chunks, counts):
    out_shape = tuple(jax.ShapeDtypeStruct((n, *chunks.shape[1:]), chunks.dtype) for n in counts)
    return kernel_call(pick_kernel, out_shape, (index,), (chunks,), "pick")


def merge_kernel(kinds, column, where, *refs):
    n = len(kinds)
    sources, spare, out, sem = refs[:n], refs[n:-2], refs[-2], refs[-1]

    @pl.loop(0, PLANE)
    def _(d):
        kind, slot = where[0, d], where[1, d]
        for i, (number, source) in enumerate(zip(kinds, sources)):
            count = source.shape[0]

            @pl.when((kind == number) & (slot < count))
            def _(source=source):
                out[d] = source[slot]

            if number:

                @pl.when((kind == number) & (slot >= count))
                def _(source=spare[i - 1], count=count):
                    columns = pl.ds(column, out.shape[2])
                    copy = pltpu.make_async_copy(
                        source.at[slot - count, :, columns], out.at[d], sem
                    )
                    copy.start()
                    copy.wait()


def merge(where, sources, spare, column):
    share = sources[0]
    kernel = functools.partial(merge_kernel, tuple(sources), column)
    out_shape = (jax.ShapeDtypeStruct(share.shape, share.dtype),)
    args = (*sources.values(), *(spare[k] for k in sources if k))
    scratch = [pltpu.SemaphoreType.DMA]
    return kernel_call(kernel, out_shape, (where,), args, "merge", len(spare), scratch)[0]


def room(n, like):
    return pl.pallas_call(
        lambda out: None,
        out_shape=jax.ShapeDtypeStruct((PLANE - n, *like), jnp.bfloat16),
        out_specs=pl.BlockSpec(memory_space=pl.ANY),
        name="room",
    )()


def step_by(n):
    return [(i, (i + n) % PLANES) for i in range(PLANES)]


def hop(sends):
    steps = {3: 1, 1: -1, 2: 2}
    return {k: lax.ppermute(s, "h", step_by(steps[k])) for k, s in sends.items()}


def depart(index, share):
    return dict(zip((3, 1, 2), pick(index, share, (NEXT, NEXT, FAR))))


def pick_late_kernel(index, *refs):
    outs = refs[-index.shape[0] :]
    for o, out in enumerate(outs):
        at = 0
        for share in refs[: -len(outs)]:
            width = share.shape[2]
            out[0, :, at : at + width] = share[index[o, 0]]
            at += width


def late(route, shares, after):
    send_index, _, next_trips, far_trips = route
    start, _ = lax.optimization_barrier((jnp.int32(0), after))
    depth, width = shares[0].shape[1], sum(s.shape[2] for s in shares)

    def trip(first, steps, slots):
        def one(state):
            i, came = state
            index = lax.dynamic_slice(send_index, (first, slots + i), (len(steps), 1))
            one_chunk = jax.ShapeDtypeStruct((1, depth, width), shares[0].dtype)
            sends = kernel_call(
                pick_late_kernel, (one_chunk,) * len(steps), (index,), shares, "pick"
            )
            new = hop(dict(zip(steps, sends)))
            return i + 1, {
                k: lax.dynamic_update_slice(old, new[k], (i, 0, 0)) for k, old in came.items()
            }

        return one

    _, near = lax.while_loop(
        lambda s: s[0] < next_trips,
        trip(0, (3, 1), NEXT),
        (start, {1: room(NEXT, (depth, width)), 3: room(NEXT, (depth, width))}),
    )
    start, _ = lax.optimization_barrier((start, near))
    _, far = lax.while_loop(
        lambda s: s[0] < far_trips, trip(2, (2,), FAR), (start, {2: room(FAR, (depth, width))})
    )
    return {**near, **far}


def over_plane(chunks):
    return lax.all_to_all(chunks, FLAT, 0, 0, tiled=True)


def swap(route, arrays):
    tie = lax.optimization_barrier
    shares, sent, came, done = [], [], [], []
    for a in arrays:
        a = a.reshape(PLANE, a.shape[0] // PLANE, a.shape[1])
        if shares:
            a, _ = tie((a, shares[-1]))
        shares.append(over_plane(a))
        sent.append(depart(route[0], shares[-1]))
        came.append(hop(sent[-1]))
    spare, column, placed = late(route, shares, (sent, came[0])), 0, []
    for share, parts in zip(shares, came):
        parts, spare = tie((parts, spare))
        placed.append(merge(route[1], {0: share, **parts}, spare, column))
        column += share.shape[2]
    placed[0], _ = tie((placed[0], (came[0], came[1][1], came[1][3])))
    done = [over_plane(p) for p in placed]
    return [d.reshape(a.shape) for d, a in zip(done, arrays)]


rows = (((0,), (0,)), ((), ()))


def grad(a, b):
    return lax.dot_general(a, b, rows, preferred_element_type=jnp.float32)


def local_step(weights, inputs, in_cols, out_cols):
    both, down = weights
    pre = jnp.dot(inputs, both, preferred_element_type=jnp.float32) * IN_SCALE
    gate_pre, up_value = pre[:, :HID], pre[:, HID:]
    sigmoid_gate = jax.nn.sigmoid(gate_pre)
    active = gate_pre * sigmoid_gate
    hidden = (active * up_value).astype(jnp.bfloat16)
    term = (
        lax.dot_general(hidden, down, (((1,), (1,)), ((), ())), preferred_element_type=jnp.float32)
        * HID_SCALE
    )
    blocks = term.astype(jnp.bfloat16).reshape(-1, N_TENSOR, COLS).transpose(1, 0, 2)
    terms = lax.all_to_all(blocks, TENSOR, 0, 0, tiled=True)
    branch = jnp.sum(terms.astype(jnp.float32), axis=0)
    error_cols = (in_cols.astype(jnp.float32) + branch - out_cols.astype(jnp.float32)).astype(
        jnp.bfloat16
    )
    errors = lax.all_gather(error_cols, TENSOR, axis=1, tiled=True)
    back = jnp.dot(errors, down, preferred_element_type=jnp.float32) * HID_SCALE
    delta_gate = back * up_value * sigmoid_gate * (1.0 + gate_pre * (1.0 - sigmoid_gate))
    delta_up = back * active
    deltas = jnp.concatenate([delta_gate, delta_up], axis=1).astype(jnp.bfloat16)
    gradients = (grad(inputs, deltas) * IN_SCALE, grad(errors, hidden) * HID_SCALE)
    return tuple(
        (w.astype(jnp.float32) - inner_rate * g).astype(jnp.bfloat16)
        for w, g in zip(weights, gradients)
    )


def partner_copy(route, arrays):
    return swap(route, arrays[::-1])[::-1]


def outer_update(weight, stepped, partner_step):
    weight = weight.astype(jnp.float32)
    pair_mean = 0.5 * (stepped.astype(jnp.float32) + partner_step.astype(jnp.float32))
    outer_grad = weight - pair_mean
    moment_new = outer_grad
    updated = weight - outer_rate * (momentum_rate * moment_new + outer_grad)
    return updated.astype(jnp.bfloat16), moment_new.astype(jnp.bfloat16)


def make_share(stepped, moment):
    return (0.475 * stepped.astype(jnp.float32) - 0.2025 * moment.astype(jnp.float32)).astype(
        jnp.bfloat16
    )


def final_update(weight, stepped, moment, partner_share):
    updated = (
        0.05 * weight.astype(jnp.float32)
        + 0.475 * stepped.astype(jnp.float32)
        - 0.2025 * moment.astype(jnp.float32)
        + partner_share.astype(jnp.float32)
    )
    return updated.astype(jnp.bfloat16)


def body(w_gate, w_up, w_down, pool, rows_index, partners):
    weights = (jnp.concatenate([w_gate[0], w_up[0]], axis=1), w_down[0].T)
    first, last = routes(partners)
    picked = jnp.take(pool[0], rows_index[0].reshape(-1), axis=0)
    picked = picked.reshape(ROUNDS, 2, -1, COLS)
    in_cols, out_cols = picked[:, 0], picked[:, 1]
    inputs = lax.all_gather(in_cols, TENSOR, axis=2, tiled=True)

    stepped = local_step(weights, inputs[0], in_cols[0], out_cols[0])
    theirs = partner_copy(first, stepped)
    results = [outer_update(*each) for each in zip(weights, stepped, theirs)]
    weights = tuple(r[0] for r in results)
    moments = tuple(r[1] for r in results)

    stepped = local_step(weights, inputs[1], in_cols[1], out_cols[1])
    shares = tuple(make_share(s, m) for s, m in zip(stepped, moments))
    theirs = partner_copy(last, shares)
    both, down = zip(weights, stepped, moments, theirs)
    gate = final_update(*(a[:, :HID] for a in both))
    up = final_update(*(a[:, HID:] for a in both))
    return gate[None], up[None], final_update(*(a.T for a in down))[None]


def solution(mesh):
    grid = Mesh(mesh.devices.reshape(4, 4, 4, 4, 2), ("x", "h", "y", "l", "c"))
    return jax.shard_map(
        body,
        mesh=grid,
        in_specs=(
            P(REPLICA, None, TENSOR),
            P(REPLICA, None, TENSOR),
            P(REPLICA, TENSOR, None),
            P(REPLICA, None, TENSOR),
            P(REPLICA, None, None, None),
            P(),
        ),
        out_specs=(
            P(REPLICA, None, TENSOR),
            P(REPLICA, None, TENSOR),
            P(REPLICA, TENSOR, None),
        ),
        check_vma=False,
    )
```
